128 devices in a mesh: scan: 32 (over y, z, x_lo), beam: 4 (over x_hi, core).
Axes of the slice: x: 4 (x_hi: 2, x_lo: 2; x = x_hi * 2 + x_lo), y: 4, z: 4, core: 2. Of those that a mesh axis runs over, the one named last changes fastest.
Arguments:
- smatrix: bfloat16 [2, 1024, 2048, 128], P(None, 'beam', 'scan'), may hold values from -6 to 6
- beam_freq: int32 [2, 1024], P(None, 'beam'), may hold values from -32 to 31
- beam_amp: float32 [2, 1024], P(None, 'beam'), may hold values from -0.1875 to 0.1875
- row_offset: int32 [2048], P('scan'), may hold values from 0 to 63
- col_offset: int32 [2048], P('scan'), may hold values from 0 to 127
- counts: int32 [32], P('scan'), may hold values from 16 to 64, as said below
- amplitude: float32 [2048, 128, 128], P('scan'), may hold values from 0.25 to 2
Outputs:
- grad_smatrix: bfloat16 [2, 1024, 2048, 128], P(None, 'beam', 'scan')
The draws below stay inside these ranges and needn't reach their ends.
Inputs may be any that keep to these rules, and one draw needn't show every extreme that they name: `counts`: slots of a tile at or past its count are unused; some tile holds exactly 64 live positions.
All inputs are finite; a program needn't handle non-finite values.
Results may differ from the reference program's by a relative error of at most 0.0063.
Values may be sent and summed in bfloat16 or wider, within the bound.
No kernel may reach another device: no remote copies, remote signals or barrier semaphores. Data moves between devices by JAX's collectives and lax.ppermute only.
A program may use at most 192 MiB of HBM per device.

```python
import math
import jax
import jax.numpy as jnp
from jax import lax

WIN = 128
BEAMS = 1024
POS_DEV = 64
TY = 64
NY = 2048
POSITIONS = 2048
N_SCAN = 32


def draw_counts(key, part):
    first_key = jax.random.fold_in(key, 11)
    second_key = jax.random.fold_in(key, 12)
    values = jax.random.randint(first_key, (N_SCAN,), max(1, POS_DEV // 4), POS_DEV + 1)
    chosen = jax.random.randint(second_key, (), 0, N_SCAN)
    return jnp.where(jnp.arange(N_SCAN) == chosen, POS_DEV, values).astype(jnp.int32)


def set_ends(values, own_key, low, largest):
    longest = values.shape.index(max(values.shape))
    spots = []
    for shift in (0, 1):
        where = [jax.random.randint(jax.random.fold_in(own_key, axis), (), 0, length) for axis, length in enumerate(values.shape)]
        where[longest] = (where[longest] + shift) % values.shape[longest]
        spots.append(tuple(where))
    return values.at[spots[0]].set(low).at[spots[1]].set(largest)


def steps_of(stream_key, dims, pieces, smallest, high):
    def one(dim, parts):
        draws = jax.random.uniform(jax.random.fold_in(jax.random.fold_in(stream_key, 6), dim), (parts,), jnp.float32, smallest / len(pieces), high / len(pieces))
        return jnp.repeat(jnp.exp(draws), dims[dim] // parts).reshape((-1,) + (1,) * (len(dims) - dim - 1))

    loudness = one(*pieces[0])
    for cut in pieces[1:]:
        loudness = loudness * one(*cut)
    return loudness


def scatter_about(rng, dims, width, most, cuts=(), kind=jnp.bfloat16):
    result = width * jax.random.normal(rng, dims, jnp.float32)
    if cuts:
        result = result * steps_of(rng, dims, cuts, -0.22, 0.18)
    return jnp.clip(result, -most, most).astype(kind)


def setup_inputs(seed: int = 0) -> dict:
    key_list = jax.random.split(jax.random.key(seed), 8)
    return {
        "smatrix": scatter_about(key_list[0], (2, BEAMS, NY, WIN), 1.0, 6.0, ((1, 4), (2, 32))),
        "beam_freq": set_ends(jax.random.randint(key_list[1], (2, BEAMS), 0 - WIN // 4, WIN // 4), jax.random.fold_in(key_list[1], 1), 0 - WIN // 4, (WIN // 4) - 1).astype(jnp.int32),
        "beam_amp": scatter_about(key_list[2], (2, BEAMS), BEAMS ** -0.5, 0.1875, ((1, 4),), jnp.float32),
        "row_offset": set_ends(jax.random.randint(key_list[3], (POSITIONS,), 0, TY), jax.random.fold_in(key_list[3], 1), 0, TY - 1).astype(jnp.int32),
        "col_offset": set_ends(jax.random.randint(key_list[4], (POSITIONS,), 0, WIN), jax.random.fold_in(key_list[4], 1), 0, WIN - 1).astype(jnp.int32),
        "counts": draw_counts(jax.random.fold_in(key_list[7], 71), 0),
        "amplitude": jnp.clip(0.25 + 1.75 * jax.random.uniform(key_list[6], (POSITIONS, WIN, WIN), jnp.float32) ** steps_of(key_list[6], (POSITIONS, WIN, WIN), ((0, 32),), -0.2, 0.2), 0.25, 2.0),
    }


TWO_PI = 6.283185307179586
ETA = 0.1

def coefficients(tile_rows, tile_cols, tile_ids, beam_freq, beam_amp, strip_rows, field_rows, window):
    global_rows = tile_ids * strip_rows + tile_rows
    along_rows = beam_freq[0][None, :] * global_rows[:, None] % field_rows
    along_cols = beam_freq[1][None, :] * tile_cols[:, None] % window
    phase_turns = along_rows.astype(jnp.float32) / field_rows + along_cols.astype(jnp.float32) / window
    phase_angle = -TWO_PI * phase_turns
    cos_part = jnp.cos(phase_angle)
    sin_part = jnp.sin(phase_angle)
    coef_re = beam_amp[0][None, :] * cos_part - beam_amp[1][None, :] * sin_part
    coef_im = beam_amp[0][None, :] * sin_part + beam_amp[1][None, :] * cos_part
    return (coef_re.astype(jnp.bfloat16), coef_im.astype(jnp.bfloat16))

def forward_matrix(coef_re, coef_im):
    real_rows = jnp.concatenate([coef_re, -coef_im], axis=1)
    imag_rows = jnp.concatenate([coef_im, coef_re], axis=1)
    return jnp.concatenate([real_rows, imag_rows], axis=0)

def backward_matrix(coef_re, coef_im):
    real_rows = jnp.concatenate([coef_re.T, coef_im.T], axis=1)
    imag_rows = jnp.concatenate([-coef_im.T, coef_re.T], axis=1)
    return jnp.concatenate([real_rows, imag_rows], axis=0)

def dft_tables(window):
    counter = jnp.arange(window, dtype=jnp.int32)
    product = counter[:, None] * counter[None, :] % window
    turn_angle = product.astype(jnp.float32) * (TWO_PI / window)
    norm_scale = 1.0 / math.sqrt(window)
    return (jnp.cos(turn_angle) * norm_scale, -jnp.sin(turn_angle) * norm_scale)

def transform(real_in, imag_in, table_re, table_im):
    highest = lax.Precision.HIGHEST
    left_re = jnp.einsum('jk,qkl->qjl', table_re, real_in, precision=highest) - jnp.einsum('jk,qkl->qjl', table_im, imag_in, precision=highest)
    left_im = jnp.einsum('jk,qkl->qjl', table_re, imag_in, precision=highest) + jnp.einsum('jk,qkl->qjl', table_im, real_in, precision=highest)
    out_re = jnp.einsum('qjk,kl->qjl', left_re, table_re, precision=highest) - jnp.einsum('qjk,kl->qjl', left_im, table_im, precision=highest)
    out_im = jnp.einsum('qjk,kl->qjl', left_re, table_im, precision=highest) + jnp.einsum('qjk,kl->qjl', left_im, table_re, precision=highest)
    return (out_re, out_im)

def far_field_gradient(wave_re, wave_im, measured, live_rows, tables):
    table_re, table_im = tables
    far_re, far_im = transform(wave_re, wave_im, table_re, table_im)
    modulus = jnp.sqrt(far_re * far_re + far_im * far_im + ETA)
    keep_share = 1.0 - measured / modulus
    back_re, back_im = transform(far_re * keep_share, far_im * keep_share, table_re, -table_im)
    live_mask = live_rows[:, None, None]
    return jnp.stack([back_re * live_mask, back_im * live_mask], axis=0).astype(jnp.bfloat16)

def selection(tile_rows, window, total_rows):
    field_index = jnp.arange(total_rows, dtype=jnp.int32)
    window_index = jnp.arange(window, dtype=jnp.int32)
    target = tile_rows[:, None, None] + window_index[None, None, :]
    return (field_index[None, :, None] == target).astype(jnp.float32)

def take_window(strip_waves, tile_rows, window):
    picker = selection(tile_rows, window, strip_waves.shape[2])
    return jnp.einsum('pyj,cpyx->cpjx', picker, strip_waves.astype(jnp.float32), precision=lax.Precision.HIGHEST)

def place_rows(wave_grads, tile_rows, total_rows):
    picker = selection(tile_rows, wave_grads.shape[2], total_rows)
    placed = jnp.einsum('pyj,cpjx->cpyx', picker, wave_grads.astype(jnp.float32))
    return placed.astype(jnp.bfloat16)

def reference(smatrix, beam_freq, beam_amp, row_offset, col_offset, counts, amplitude):
    tables = dft_tables(WIN)
    field_rows = TY * N_SCAN

    def tile_coefficients(tile_id):
        tile_rows = lax.dynamic_slice_in_dim(row_offset, tile_id * POS_DEV, POS_DEV)
        tile_cols = lax.dynamic_slice_in_dim(col_offset, tile_id * POS_DEV, POS_DEV)
        tile_ids = jnp.full((POS_DEV,), tile_id, jnp.int32)
        return (tile_rows, coefficients(tile_rows, tile_cols, tile_ids, beam_freq, beam_amp, TY, field_rows, WIN))

    def strip_of(strip_index):
        return lax.dynamic_slice_in_dim(smatrix, (strip_index % N_SCAN * TY).astype(jnp.int32), TY, axis=2)

    def forward_tile(tile_id):
        tile_rows, (coef_re, coef_im) = tile_coefficients(tile_id)
        extended = jnp.concatenate([strip_of(tile_id + distance) for distance in range(3)], axis=2).reshape(2 * BEAMS, 3 * TY * WIN)
        strip_waves = jnp.dot(forward_matrix(coef_re, coef_im), extended, preferred_element_type=jnp.float32).reshape(2, POS_DEV, 3 * TY, WIN)
        windows = take_window(strip_waves, tile_rows, WIN)
        live_rows = (jnp.arange(POS_DEV, dtype=jnp.int32) < lax.dynamic_index_in_dim(counts, tile_id, keepdims=False)).astype(jnp.float32)
        measured = lax.dynamic_slice_in_dim(amplitude, tile_id * POS_DEV, POS_DEV)
        return far_field_gradient(windows[0], windows[1], measured, live_rows, tables)
    tile_list = jnp.arange(N_SCAN, dtype=jnp.int32)
    all_grads = lax.map(forward_tile, tile_list)

    def strip_gradient(strip_id):
        grad_parts = []
        re_parts = []
        im_parts = []
        for distance in range(3):
            tile_id = ((strip_id - distance) % N_SCAN).astype(jnp.int32)
            tile_rows, (coef_re, coef_im) = tile_coefficients(tile_id)
            wave_grads = lax.dynamic_index_in_dim(all_grads, tile_id, keepdims=False)
            placed = place_rows(wave_grads, tile_rows, 3 * TY)
            grad_parts.append(placed[:, :, distance * TY:(distance + 1) * TY])
            re_parts.append(coef_re)
            im_parts.append(coef_im)
        gathered = jnp.stack(grad_parts, axis=1).reshape(6 * POS_DEV, TY * WIN)
        matrix = backward_matrix(jnp.concatenate(re_parts, axis=0), jnp.concatenate(im_parts, axis=0))
        return jnp.dot(matrix, gathered, preferred_element_type=jnp.float32).astype(jnp.bfloat16).reshape(2, BEAMS, TY, WIN)
    strips = lax.map(strip_gradient, tile_list)
    return jnp.transpose(strips, (1, 2, 0, 3, 4)).reshape(2, BEAMS, N_SCAN * TY, WIN)
```

```python
import math

import jax
import jax.numpy as jnp
import ml_dtypes
import numpy as np
from jax import lax
from jax.experimental import pallas as pl
from jax.experimental.pallas import tpu as pltpu
from jax.sharding import PartitionSpec as P

TWO_PI = 6.283185307179586
ETA = 0.1
BF16 = jnp.bfloat16
F32 = jnp.float32
AXES = ("scan", "beam")
Y_BLOCK = 16


def permutation(scan_size, target):
    pairs = []
    for s in range(scan_size):
        for hi in range(2):
            for core in range(2):
                ts, th, tc = target(s, hi, core)
                pairs.append(((s * 2 + hi) * 2 + core, ((ts % scan_size) * 2 + th) * 2 + tc))
    return pairs


def coefficients(rows, cols, ids, beam_freq, beam_amp, strip_rows, field_rows, window):
    global_rows = ids * strip_rows + rows
    along_rows = beam_freq[0][None, :] * global_rows[:, None] % field_rows
    along_cols = beam_freq[1][None, :] * cols[:, None] % window
    phase_turns = (
        along_rows.astype(F32) / field_rows + along_cols.astype(F32) / window
    )
    phase_angle = -TWO_PI * phase_turns
    cos_part = jnp.cos(phase_angle)
    sin_part = jnp.sin(phase_angle)
    coef_re = beam_amp[0][None, :] * cos_part - beam_amp[1][None, :] * sin_part
    coef_im = beam_amp[0][None, :] * sin_part + beam_amp[1][None, :] * cos_part
    return (coef_re.astype(BF16), coef_im.astype(BF16))


def dft_matrices(window):
    counter = np.arange(window)
    angle = (counter[:, None] * counter[None, :] % window) * (2.0 * math.pi / window)
    re = np.cos(angle) / math.sqrt(window)
    im = -np.sin(angle) / math.sqrt(window)
    full = np.block([[re, im], [-im, re]])
    high = full.astype(ml_dtypes.bfloat16)
    low = (full - high.astype(np.float64)).astype(ml_dtypes.bfloat16)
    return np.stack([high, low, high.T, low.T])


def split(value):
    high = value.astype(BF16)
    return high, (value - high.astype(F32)).astype(BF16)


def dot(left, right):
    return jnp.dot(left, right, preferred_element_type=F32)


def right_product(value, high, low):
    value_hi, value_lo = split(value)
    return dot(value_hi, high) + (dot(value_lo, high) + dot(value_hi, low))


def left_product(high, low, value):
    value_hi, value_lo = split(value)
    return dot(high, value_hi) + (dot(high, value_lo) + dot(low, value_hi))


def forward_kernel(coef_ref, field_ref, *out_refs):
    parts = field_ref.shape[0]
    beams = field_ref.shape[1]
    field = field_ref[...].reshape(parts * beams, Y_BLOCK, field_ref.shape[3])
    by_row = jnp.swapaxes(field, 0, 1)
    for y in range(Y_BLOCK):
        waves = dot(coef_ref[...], by_row[y]).astype(BF16)
        start = 0
        for out_ref in out_refs:
            rows = out_ref.shape[1]
            out_ref[y] = waves[start : start + rows]
            start += rows


def forward_waves(coef, smatrix, groups):
    parts, beams, strip_rows, window = smatrix.shape
    total = coef.shape[0]
    rows = total // groups
    return pl.pallas_call(
        forward_kernel,
        grid=(strip_rows // Y_BLOCK,),
        in_specs=[
            pl.BlockSpec((total, parts * beams), lambda i: (0, 0)),
            pl.BlockSpec((parts, beams, Y_BLOCK, window), lambda i: (0, 0, i, 0)),
        ],
        out_specs=[pl.BlockSpec((Y_BLOCK, rows, window), lambda i: (i, 0, 0))] * groups,
        out_shape=[jax.ShapeDtypeStruct((strip_rows, rows, window), BF16)] * groups,
        compiler_params=pltpu.CompilerParams(vmem_limit_bytes=50 << 20),
        cost_estimate=pl.CostEstimate(
            flops=2 * total * parts * beams * strip_rows * window,
            bytes_accessed=2 * (parts * beams + total) * strip_rows * window,
            transcendentals=0,
        ),
        name="forward_waves",
    )(coef, smatrix)


def backward_kernel(coef_ref, low_ref, high_ref, *refs):
    wave_refs, out_ref = refs[:-1], refs[-1]
    parts, beams = out_ref.shape[0], out_ref.shape[1]
    first = pl.program_id(0) * Y_BLOCK
    low, high = low_ref[...], high_ref[...]
    rows = []
    for y in range(Y_BLOCK):
        waves = jnp.concatenate([ref[y] for ref in wave_refs], axis=0)
        row = (first + y).astype(F32)
        keep = jnp.logical_and(low <= row, row < high)
        waves = jnp.where(keep, waves, jnp.zeros_like(waves))
        rows.append(dot(coef_ref[...], waves).astype(BF16))
    by_row = jnp.stack(rows, axis=0)
    out_ref[...] = jnp.swapaxes(by_row, 0, 1).reshape(parts, beams, Y_BLOCK, by_row.shape[2])


def backward_gradient(coef_t, low, high, pieces, parts, beams):
    strip_rows, rows, window = pieces[0].shape
    total = coef_t.shape[1]
    return pl.pallas_call(
        backward_kernel,
        grid=(strip_rows // Y_BLOCK,),
        in_specs=[
            pl.BlockSpec((parts * beams, total), lambda i: (0, 0)),
            pl.BlockSpec((total, window), lambda i: (0, 0)),
            pl.BlockSpec((total, window), lambda i: (0, 0)),
        ]
        + [pl.BlockSpec((Y_BLOCK, rows, window), lambda i: (i, 0, 0))] * len(pieces),
        out_specs=pl.BlockSpec((parts, beams, Y_BLOCK, window), lambda i: (0, 0, i, 0)),
        out_shape=jax.ShapeDtypeStruct((parts, beams, strip_rows, window), BF16),
        compiler_params=pltpu.CompilerParams(vmem_limit_bytes=50 << 20),
        cost_estimate=pl.CostEstimate(
            flops=2 * total * parts * beams * strip_rows * window,
            bytes_accessed=2 * (parts * beams + total) * strip_rows * window,
            transcendentals=0,
        ),
        name="backward_gradient",
    )(coef_t, low, high, *pieces)


def far_kernel(table_ref, amp_ref, live_ref, a0_ref, a1_ref, b0_ref, b1_ref, ga_ref, gb_ref, mid, back):
    half, both, window = a0_ref.shape
    count = both // 2
    fwd_hi, fwd_lo = table_ref[0], table_ref[1]
    inv_hi, inv_lo = table_ref[2], table_ref[3]
    for k, (x_ref, y_ref) in enumerate(((a0_ref, a1_ref), (b0_ref, b1_ref))):
        total = x_ref[...].astype(F32) + y_ref[...].astype(F32)
        pair = jnp.concatenate([total[:, :count], total[:, count:]], axis=2)
        out = right_product(pair.reshape(half * count, 2 * window), fwd_hi, fwd_lo)
        out = jnp.swapaxes(out.reshape(half, count, 2 * window), 0, 1)
        mid[:, k * half : (k + 1) * half, :] = out

    def one_pair(step, carry):
        first = step * 2
        stacked = []
        for p in range(2):
            rows = mid[first + p]
            stacked.append(jnp.concatenate([rows[:, :window], rows[:, window:]], axis=0))
        far = left_product(inv_hi, inv_lo, jnp.concatenate(stacked, axis=1))
        far_re, far_im = far[: 2 * half], far[2 * half :]
        measured = jnp.concatenate([amp_ref[first], amp_ref[first + 1]], axis=1).astype(F32)
        keep = 1.0 - measured * lax.rsqrt(far_re * far_re + far_im * far_im + ETA)
        residual = jnp.concatenate([far_re * keep, far_im * keep], axis=0)
        grad = left_product(fwd_hi, fwd_lo, residual)
        for p in range(2):
            lanes = slice(p * window, (p + 1) * window)
            pair = jnp.concatenate([grad[: 2 * half, lanes], grad[2 * half :, lanes]], axis=1)
            back[first + p] = pair
        return carry

    lax.fori_loop(0, count // 2, one_pair, 0, unroll=2)
    for k, g_ref in enumerate((ga_ref, gb_ref)):
        rows = back[:, k * half : (k + 1) * half, :]
        out = right_product(rows.reshape(count * half, 2 * window), inv_hi, inv_lo)
        out = out.reshape(count, half, 2 * window) * live_ref[...][:, :, :1]
        out = jnp.swapaxes(out, 0, 1)
        g_ref[:, :count, :] = out[:, :, :window].astype(BF16)
        g_ref[:, count:, :] = out[:, :, window:].astype(BF16)


def far_gradient(tables, amplitude, live, pieces):
    half, both, window = pieces[0].shape
    count = both // 2
    shape = jax.ShapeDtypeStruct((half, both, window), BF16)
    return pl.pallas_call(
        far_kernel,
        out_shape=[shape, shape],
        scratch_shapes=[
            pltpu.VMEM((count, 2 * half, 2 * window), F32),
            pltpu.VMEM((count, 2 * half, 2 * window), F32),
        ],
        compiler_params=pltpu.CompilerParams(vmem_limit_bytes=50 << 20),
        cost_estimate=pl.CostEstimate(
            flops=12 * 2 * count * 2 * half * 4 * window * window,
            bytes_accessed=16 * half * both * window,
            transcendentals=count * window * window,
        ),
        name="far_gradient",
    )(tables, amplitude, live, *pieces)


def body(smatrix, beam_freq, beam_amp, row_offset, col_offset, counts, amplitude):
    parts, beams, strip_rows, window = smatrix.shape
    per_tile = row_offset.shape[0]
    quarter = per_tile // 4
    scan_size = lax.axis_size("scan")
    field_rows = strip_rows * scan_size
    me = lax.axis_index("scan")
    beam_at = lax.axis_index("beam")
    hi, core = beam_at // 2, beam_at % 2
    odd = me % 2 == 1

    def send(value, target):
        return lax.ppermute(value, AXES, permutation(scan_size, target))

    def to_core(value):
        return send(value, lambda s, h, c: (s, h, 1 - c))

    def to_hi(value):
        return send(value, lambda s, h, c: (s, 1 - h, c))

    def to_near(value):
        return send(value, lambda s, h, c: (s ^ 1, h, c))

    def to_cross(value):
        return send(value, lambda s, h, c: (s ^ 1, 1 - h, c))

    def to_owner(value):
        return send(value, lambda s, h, c: (s + 2 if s % 2 else s - 2, h, c))

    def to_strip(value):
        return send(value, lambda s, h, c: (s - 2 if s % 2 else s + 2, h, c))

    packed = jnp.concatenate([row_offset, col_offset, jnp.broadcast_to(counts, (per_tile,))])
    before_1 = send(packed, lambda s, h, c: (s + 1, h, c))
    before_2 = send(packed, lambda s, h, c: (s + 2, h, c))
    first = core * (2 * quarter) + hi * quarter
    own_amp = lax.dynamic_slice_in_dim(amplitude, first, quarter, 0)
    odd_pairs = [
        pair
        for pair in permutation(scan_size, lambda s, h, c: (s + 2, h, c))
        if (pair[0] // 4) % 2
    ]
    moved_amp = lax.ppermute(own_amp.astype(BF16), AXES, odd_pairs)
    my_amp = jnp.where(odd, moved_amp.astype(F32), own_amp)

    local = jnp.where(odd, before_2, packed)
    remote = jnp.where(odd, packed, before_2)
    middle = before_1
    local_id = jnp.where(odd, me - 2, me) % scan_size
    remote_id = jnp.where(odd, me, me - 2) % scan_size
    middle_id = (me - 1) % scan_size

    def ordered(values):
        grid = values.reshape(2, 2, quarter)
        grid = jnp.where(core == 1, grid[::-1], grid)
        return jnp.where(hi == 1, grid[:, ::-1], grid)

    rows, cols, ids = [], [], []
    for tile, tile_id in ((remote, remote_id), (local, local_id), (middle, middle_id)):
        rows.append(ordered(tile[:per_tile]))
        cols.append(ordered(tile[per_tile : 2 * per_tile]))
        ids.append(jnp.full((2, 2, quarter), tile_id, jnp.int32))
    rows = jnp.stack(rows, axis=1)
    cols = jnp.stack(cols, axis=1)
    ids = jnp.stack(ids, axis=1)
    flat = 3 * per_tile
    coef_re, coef_im = coefficients(
        rows.reshape(flat), cols.reshape(flat), ids.reshape(flat),
        beam_freq, beam_amp, strip_rows, field_rows, window,
    )
    blocks = flat // quarter
    coef_re = coef_re.reshape(blocks, 1, quarter, beams)
    coef_im = coef_im.reshape(blocks, 1, quarter, beams)
    coef = jnp.concatenate(
        [
            jnp.concatenate([coef_re, -coef_im], axis=3),
            jnp.concatenate([coef_im, coef_re], axis=3),
        ],
        axis=1,
    ).reshape(2 * flat, parts * beams)

    zero = jnp.zeros_like(rows[:, 0])
    top = jnp.full_like(zero, strip_rows)
    low = jnp.stack(
        [jnp.where(odd, rows[:, 0], zero), jnp.where(odd, zero, rows[:, 1]), zero], axis=1
    )
    high = jnp.stack(
        [jnp.where(odd, top, rows[:, 0]), jnp.where(odd, rows[:, 1], top), top], axis=1
    )

    def per_row(values):
        values = jnp.broadcast_to(values[:, :, :, None, :], (2, 3, 2, 2, quarter))
        return values.reshape(2 * flat)

    low, high = per_row(low), per_row(high)

    mine_rem, mine_loc, mine_mid, other_rem, other_loc, other_mid = forward_waves(coef, smatrix, 6)
    unit = 2 * quarter

    def joined(mine, other):
        return mine.astype(F32) + to_core(other).astype(F32)

    sum_rem = joined(mine_rem, other_rem).astype(BF16)
    from_rem = to_owner(sum_rem)
    sum_mid = joined(mine_mid, other_mid).astype(BF16)
    near_mid = to_near(sum_mid[:, :unit])
    cross_mid = to_cross(sum_mid[:, unit:])
    sum_loc = joined(mine_loc, other_loc)
    y_index = jnp.arange(strip_rows, dtype=jnp.int32)[:, None]
    inside = jnp.logical_and(
        low[None, 2 * unit : 4 * unit] <= y_index, y_index < high[None, 2 * unit : 4 * unit]
    )
    window_a = jnp.where(inside[:, :, None], sum_loc, from_rem.astype(F32)).astype(BF16)
    other_a = to_hi(window_a[:, unit:])
    own_a = window_a[:, :unit]

    own_count = local[2 * per_tile]
    live = (first + jnp.arange(quarter, dtype=jnp.int32) < own_count).astype(F32)
    live = jnp.broadcast_to(live[:, None, None], (quarter, 1, window))
    tables = jnp.asarray(dft_matrices(window))
    grad_a, grad_b = far_gradient(tables, my_amp, live, (own_a, other_a, near_mid, cross_mid))

    grad_a_hi = to_hi(grad_a)
    pieces = [
        to_strip(grad_a), to_strip(grad_a_hi),
        grad_a, grad_a_hi,
        to_near(grad_b), to_cross(grad_b),
    ]
    pieces = pieces + [to_core(piece) for piece in pieces]
    low = jnp.broadcast_to(low.astype(F32)[:, None], (2 * flat, window))
    high = jnp.broadcast_to(high.astype(F32)[:, None], (2 * flat, window))
    return backward_gradient(coef.T, low, high, pieces, parts, beams)


def solution(mesh):
    return jax.shard_map(
        body,
        mesh=mesh,
        in_specs=(
            P(None, "beam", "scan", None),
            P(None, "beam"),
            P(None, "beam"),
            P("scan"),
            P("scan"),
            P("scan"),
            P("scan", None, None),
        ),
        out_specs=P(None, "beam", "scan", None),
        check_vma=False,
    )
```

```python
import functools
import math

import jax
import jax.numpy as jnp
import ml_dtypes
import numpy as np
from jax import lax
from jax.experimental import pallas as pl
from jax.experimental.pallas import tpu as pltpu
from jax.sharding import PartitionSpec as P

TWO_PI = 6.283185307179586
ETA = 0.1
BF16 = jnp.bfloat16
F32 = jnp.float32
AXES = ("scan", "beam")
Y_BLOCK = 16


def permutation(scan_size, target):
    pairs = []
    for s in range(scan_size):
        for hi in range(2):
            for core in range(2):
                ts, th, tc = target(s, hi, core)
                pairs.append(((s * 2 + hi) * 2 + core, ((ts % scan_size) * 2 + th) * 2 + tc))
    return pairs


def coefficient_kernel(
    where_ref, here_ref, before_1_ref, before_2_ref, freq_ref, amp_ref,
    rem_ref, rest_ref, low_ref, high_ref, live_ref,
):
    me, odd, core, hi, tiles = (where_ref[k] for k in range(5))
    per_tile = here_ref.shape[1]
    quarter = per_tile // 4
    beams = freq_ref.shape[1]
    window = low_ref.shape[1]
    strip_rows = window // 2
    field_rows = tiles * strip_rows
    is_odd = odd == 1
    here, before_1, before_2 = here_ref[...], before_1_ref[...], before_2_ref[...]
    remote = jnp.where(is_odd, here, before_2)
    local = jnp.where(is_odd, before_2, here)
    back = 2 * odd
    parts = ((remote, me - 2 + back), (local, me - back), (before_1, me - 1))
    lane = lax.broadcasted_iota(jnp.int32, (quarter, per_tile), 1)
    index = lax.broadcasted_iota(jnp.int32, (quarter, per_tile), 0)
    step = 2 * quarter
    for part, (tile, tile_id) in enumerate(parts):
        for block in range(4):
            first = jnp.bitwise_xor(core, block // 2) * step + jnp.bitwise_xor(hi, block % 2) * quarter
            chosen = lane == first + index
            row = jnp.sum(jnp.where(chosen, tile[0:1], 0), axis=1, keepdims=True)
            col = jnp.sum(jnp.where(chosen, tile[1:2], 0), axis=1, keepdims=True)
            global_row = tile_id * strip_rows + row
            along_rows = jnp.bitwise_and(freq_ref[0:1] * global_row, field_rows - 1)
            along_cols = jnp.bitwise_and(freq_ref[1:2] * col, window - 1)
            turns = along_rows.astype(F32) / field_rows.astype(F32) + along_cols.astype(F32) / window
            angle = -TWO_PI * turns
            cos_part, sin_part = jnp.cos(angle), jnp.sin(angle)
            re = amp_ref[0:1] * cos_part - amp_ref[1:2] * sin_part
            im = amp_ref[0:1] * sin_part + amp_ref[1:2] * cos_part
            re, im = re.astype(BF16), im.astype(BF16)
            out_ref = rest_ref if part else rem_ref
            start = ((part - 1) * 4 if part else 0) * step + block * step
            out_ref[start : start + quarter, :beams] = re
            out_ref[start : start + quarter, beams:] = -im
            out_ref[start + quarter : start + step, :beams] = im
            out_ref[start + quarter : start + step, beams:] = re
            row = jnp.broadcast_to(row.astype(F32), (quarter, window))
            none, full = jnp.zeros_like(row), jnp.full_like(row, strip_rows)
            from_row = is_odd if part == 0 else jnp.logical_not(is_odd)
            if part == 2:
                low, high = none, full
            else:
                low, high = jnp.where(from_row, row, none), jnp.where(from_row, full, row)
            start = (part * 4 + block) * step
            for copy in range(2):
                at = start + copy * quarter
                low_ref[at : at + quarter] = low
                high_ref[at : at + quarter] = high
    first = core * step + hi * quarter
    position = lax.broadcasted_iota(jnp.int32, (quarter, window), 0) + first
    live_ref[...] = (position < local[2:3, :1]).astype(F32)


def coefficients(where, here, before_1, before_2, beam_freq, beam_amp, parts, window):
    beams = beam_freq.shape[1]
    per_tile = here.shape[1]
    shapes = [
        jax.ShapeDtypeStruct((2 * per_tile, parts * beams), BF16),
        jax.ShapeDtypeStruct((4 * per_tile, parts * beams), BF16),
        jax.ShapeDtypeStruct((6 * per_tile, window), F32),
        jax.ShapeDtypeStruct((6 * per_tile, window), F32),
        jax.ShapeDtypeStruct((per_tile // 4, window), F32),
    ]
    return pl.pallas_call(
        coefficient_kernel,
        in_specs=[pl.BlockSpec(memory_space=pltpu.SMEM)]
        + [pl.BlockSpec(memory_space=pltpu.VMEM)] * 5,
        out_specs=[pl.BlockSpec(memory_space=pltpu.VMEM)] * 5,
        out_shape=shapes,
        compiler_params=pltpu.CompilerParams(vmem_limit_bytes=16 << 20),
        name="coefficients",
    )(where, here, before_1, before_2, beam_freq, beam_amp)


def dft_matrices(window):
    counter = np.arange(window)
    angle = (counter[:, None] * counter[None, :] % window) * (2.0 * math.pi / window)
    re = np.cos(angle) / math.sqrt(window)
    im = -np.sin(angle) / math.sqrt(window)
    full = np.block([[re, im], [-im, re]])
    high = full.astype(ml_dtypes.bfloat16)
    low = (full - high.astype(np.float64)).astype(ml_dtypes.bfloat16)
    return np.stack([high, low, high.T, low.T])


def split(value):
    high = value.astype(BF16)
    return high, (value - high.astype(F32)).astype(BF16)


def dot(left, right):
    return jnp.dot(left, right, preferred_element_type=F32)


def right_product(value, high, low):
    value_hi, value_lo = split(value)
    return dot(value_hi, high) + (dot(value_lo, high) + dot(value_hi, low))


def left_product(high, low, value):
    value_hi, value_lo = split(value)
    return dot(high, value_hi) + (dot(high, value_lo) + dot(low, value_hi))


def transpose_kernel(at_ref, field_ref, amp_ref, out_ref, own_ref, sent_ref):
    parts, beams, rows, window = field_ref.shape
    out_ref[...] = jnp.swapaxes(field_ref[...].reshape(parts * beams, rows, window), 0, 1)
    own_ref[...] = amp_ref[...]
    sent_ref[...] = amp_ref[...].astype(BF16)


def rows_first(at, smatrix, amplitude):
    parts, beams, strip_rows, window = smatrix.shape
    blocks = strip_rows // Y_BLOCK
    quarter = amplitude.shape[0] // 4
    each = quarter // (blocks * parts)
    amp_block = (each, *amplitude.shape[1:])
    amp_out = pl.BlockSpec(amp_block, lambda i, p, at: (i * parts + p, 0, 0))
    return pl.pallas_call(
        transpose_kernel,
        grid_spec=pltpu.PrefetchScalarGridSpec(
            num_scalar_prefetch=1,
            grid=(blocks, parts),
            in_specs=[
                pl.BlockSpec((1, beams, Y_BLOCK, window), lambda i, p, at: (p, 0, i, 0)),
                pl.BlockSpec(
                    amp_block, lambda i, p, at: (at[0] * (blocks * parts) + i * parts + p, 0, 0)
                ),
            ],
            out_specs=[
                pl.BlockSpec((Y_BLOCK, beams, window), lambda i, p, at: (i, p, 0)),
                amp_out,
                amp_out,
            ],
        ),
        out_shape=[
            jax.ShapeDtypeStruct((strip_rows, parts * beams, window), BF16),
            jax.ShapeDtypeStruct((quarter, *amplitude.shape[1:]), F32),
            jax.ShapeDtypeStruct((quarter, *amplitude.shape[1:]), BF16),
        ],
        compiler_params=pltpu.CompilerParams(vmem_limit_bytes=24 << 20),
        cost_estimate=pl.CostEstimate(
            flops=0, bytes_accessed=4 * parts * beams * strip_rows * window, transcendentals=0
        ),
        name="rows_first",
    )(at, smatrix, amplitude)


def forward_kernel(rem_ref, rest_ref, field_ref, *out_refs):
    coef = jnp.concatenate([rem_ref[...], rest_ref[...]], axis=0)
    for y in range(field_ref.shape[0]):
        waves = dot(coef, field_ref[y]).astype(BF16)
        start = 0
        for out_ref in out_refs:
            rows = out_ref.shape[1]
            out_ref[y] = waves[start : start + rows]
            start += rows


def forward_waves(coefs, field):
    strip_rows, depth, window = field.shape
    total = sum(coef.shape[0] for coef in coefs)
    rows = total // 6
    block = Y_BLOCK // 2
    return pl.pallas_call(
        forward_kernel,
        grid=(strip_rows // block,),
        in_specs=[pl.BlockSpec(coef.shape, lambda i: (0, 0)) for coef in coefs]
        + [pl.BlockSpec((block, depth, window), lambda i: (i, 0, 0))],
        out_specs=[pl.BlockSpec((block, rows, window), lambda i: (i, 0, 0))] * 6,
        out_shape=[jax.ShapeDtypeStruct((strip_rows, rows, window), BF16)] * 6,
        compiler_params=pltpu.CompilerParams(vmem_limit_bytes=16 << 20),
        cost_estimate=pl.CostEstimate(
            flops=2 * total * depth * strip_rows * window,
            bytes_accessed=2 * (depth + total) * strip_rows * window,
            transcendentals=0,
        ),
        name="forward_waves",
    )(*coefs, field)


def backward_kernel(first_row, has_before, rem_ref, rest_ref, low_ref, high_ref, *refs):
    refs = refs[2:] if has_before else refs
    wave_refs, out_ref, done_ref, turned = refs[:-3], refs[-3], refs[-2], refs[-1]
    done_ref[...] = jnp.zeros_like(done_ref)
    parts, beams = out_ref.shape[0], out_ref.shape[1]
    split_at = rem_ref.shape[0]

    @pl.when(pl.program_id(0) == 0)
    def turn():
        turned[:, :split_at] = rem_ref[...].T
        turned[:, split_at:] = rest_ref[...].T

    first = pl.program_id(0) * Y_BLOCK + first_row
    low, high = low_ref[...], high_ref[...]
    rows = []
    for y in range(Y_BLOCK):
        waves = jnp.concatenate([ref[y] for ref in wave_refs], axis=0)
        row = (first + y).astype(F32)
        keep = jnp.logical_and(low <= row, row < high)
        waves = jnp.where(keep, waves, jnp.zeros_like(waves))
        rows.append(dot(turned[...], waves).astype(BF16))
    by_row = jnp.stack(rows, axis=0)
    out_ref[...] = jnp.swapaxes(by_row, 0, 1).reshape(parts, beams, Y_BLOCK, by_row.shape[2])


def backward_gradient(coefs, low, high, pieces, parts, beams, first_row, strip_rows, before):
    rows, window = pieces[0].shape[1:]
    part_rows = strip_rows // 2
    total = low.shape[0]
    offset = first_row // Y_BLOCK
    kept = [] if before is None else [*before]

    def piece_spec(piece):
        skip = offset if piece.shape[0] == strip_rows else 0
        return pl.BlockSpec((Y_BLOCK, rows, window), lambda i: (i + skip, 0, 0))

    def whole(value):
        return pl.BlockSpec(value.shape, lambda i: (0, 0))

    return pl.pallas_call(
        functools.partial(backward_kernel, first_row, before is not None),
        grid=(part_rows // Y_BLOCK,),
        in_specs=[whole(value) for value in (*coefs, low, high)]
        + [pl.BlockSpec(memory_space=pl.ANY)] * len(kept)
        + [piece_spec(piece) for piece in pieces],
        out_specs=[
            pl.BlockSpec((parts, beams, Y_BLOCK, window), lambda i: (0, 0, i + offset, 0)),
            pl.BlockSpec((8, window), lambda i: (0, 0)),
        ],
        out_shape=[
            jax.ShapeDtypeStruct((parts, beams, strip_rows, window), BF16),
            jax.ShapeDtypeStruct((8, window), F32),
        ],
        scratch_shapes=[pltpu.VMEM((parts * beams, total), BF16)],
        input_output_aliases={4: 0} if kept else {},
        compiler_params=pltpu.CompilerParams(vmem_limit_bytes=32 << 20),
        cost_estimate=pl.CostEstimate(
            flops=2 * total * parts * beams * part_rows * window,
            bytes_accessed=2 * (parts * beams + total) * part_rows * window,
            transcendentals=0,
        ),
        name=f"backward_gradient_{first_row}",
    )(*coefs, low, high, *kept, *pieces)


def far_kernel(
    table_ref, amp_ref, moved_ref, odd_ref, live_ref, low_ref, high_ref, mine_ref, got_ref,
    top_rem_ref, top_got_ref, end_got_ref, end_rem_ref, near_ref, cross_ref,
    ga_top_ref, ga_end_ref, ga_ref, gb_ref, mid, back,
):
    half, both, window = near_ref.shape
    part = half // 2
    count = both // 2
    fwd_hi, fwd_lo = table_ref[0], table_ref[1]
    inv_hi, inv_lo = table_ref[2], table_ref[3]
    own = mine_ref[...].astype(F32) + got_ref[...].astype(F32)
    row = lax.broadcasted_iota(jnp.int32, own.shape, 0).astype(F32)
    inside = jnp.logical_and(low_ref[...][None] <= row, row < high_ref[...][None])
    top = jnp.where(inside[:part], own[:part], top_rem_ref[...].astype(F32))
    top = top + top_got_ref[...].astype(F32)
    end = own[part:] + end_got_ref[...].astype(F32)
    end = jnp.where(inside[part:], end, end_rem_ref[...].astype(F32))
    middle = near_ref[...].astype(F32) + cross_ref[...].astype(F32)
    for first, total in ((0, top), (part, end), (half, middle)):
        rows = total.shape[0]
        pair = jnp.concatenate([total[:, :count], total[:, count:]], axis=2)
        out = right_product(pair.reshape(rows * count, 2 * window), fwd_hi, fwd_lo)
        out = jnp.swapaxes(out.reshape(rows, count, 2 * window), 0, 1)
        mid[:, first : first + rows, :] = out
    odd = jnp.broadcast_to(odd_ref[...], (2 * half, window)) > 0.0

    def amplitude(p):
        return jnp.where(odd, moved_ref[p].astype(F32), amp_ref[p])

    def one_pair(step, carry):
        first = step * 2
        stacked = []
        for p in range(2):
            rows = mid[first + p]
            stacked.append(jnp.concatenate([rows[:, :window], rows[:, window:]], axis=0))
        far = left_product(inv_hi, inv_lo, jnp.concatenate(stacked, axis=1))
        far_re, far_im = far[: 2 * half], far[2 * half :]
        measured = jnp.concatenate([amplitude(first), amplitude(first + 1)], axis=1)
        keep = 1.0 - measured * lax.rsqrt(far_re * far_re + far_im * far_im + ETA)
        residual = jnp.concatenate([far_re * keep, far_im * keep], axis=0)
        grad = left_product(fwd_hi, fwd_lo, residual)
        for p in range(2):
            lanes = slice(p * window, (p + 1) * window)
            pair = jnp.concatenate([grad[: 2 * half, lanes], grad[2 * half :, lanes]], axis=1)
            back[first + p] = pair
        return carry

    lax.fori_loop(0, count // 2, one_pair, 0, unroll=2)
    live = live_ref[...][:, None, :1]
    for first in range(0, 2 * half, part):
        rows = back[:, first : first + part, :]
        out = right_product(rows.reshape(count * part, 2 * window), inv_hi, inv_lo)
        out = jnp.swapaxes(out.reshape(count, part, 2 * window) * live, 0, 1)
        out_re, out_im = out[:, :, :window].astype(BF16), out[:, :, window:].astype(BF16)
        g_ref = ga_ref if first < half else gb_ref
        targets = [g_ref.at[first % half : first % half + part]]
        if first < half:
            targets.append(ga_end_ref if first else ga_top_ref)
        for target in targets:
            target[:, :count, :] = out_re
            target[:, count:, :] = out_im


def far_gradient(tables, amplitude, moved, odd, live, low, high, pieces):
    half, both, window = pieces[-1].shape
    count = both // 2
    shape = jax.ShapeDtypeStruct((half // 2, both, window), BF16)
    whole_shape = jax.ShapeDtypeStruct((half, both, window), BF16)

    def whole(value):
        return pl.BlockSpec(value.shape, lambda i: (0,) * value.ndim)

    def rows_of(value, index):
        return pl.BlockSpec((*value.shape[:-2], both, window), lambda i: index)

    mine, got, top_rem, *rest = pieces
    own_block = 4
    return pl.pallas_call(
        far_kernel,
        grid=(1,),
        in_specs=[whole(value) for value in (tables, amplitude, moved, odd, live)]
        + [rows_of(low, (own_block, 0)), rows_of(high, (own_block, 0))]
        + [rows_of(value, (0, 0, 0)) for value in (mine, got, top_rem)]
        + [whole(value) for value in rest],
        out_specs=[whole(shape), whole(shape), whole(whole_shape), whole(whole_shape)],
        out_shape=[shape, shape, whole_shape, whole_shape],
        scratch_shapes=[
            pltpu.VMEM((count, 2 * half, 2 * window), F32),
            pltpu.VMEM((count, 2 * half, 2 * window), F32),
        ],
        compiler_params=pltpu.CompilerParams(vmem_limit_bytes=36 << 20),
        cost_estimate=pl.CostEstimate(
            flops=12 * 2 * count * 2 * half * 4 * window * window,
            bytes_accessed=16 * half * both * window,
            transcendentals=count * window * window,
        ),
        name="far_gradient",
    )(tables, amplitude, moved, odd, live, low, high, *pieces)


def body(smatrix, beam_freq, beam_amp, row_offset, col_offset, counts, amplitude):
    parts, beams, strip_rows, window = smatrix.shape
    per_tile = row_offset.shape[0]
    quarter = per_tile // 4
    scan_size = lax.axis_size("scan")
    me = lax.axis_index("scan")
    beam_at = lax.axis_index("beam")
    hi, core = beam_at // 2, beam_at % 2
    at = core * 2 + hi
    odd = me % 2
    where = jnp.stack([me, odd, core, hi, jnp.int32(scan_size), at]).astype(jnp.int32)
    odd_row = jnp.broadcast_to(odd.astype(F32), (1, window))

    def send(value, target):
        return lax.ppermute(value, AXES, permutation(scan_size, target))

    def to_core(value):
        return send(value, lambda s, h, c: (s, h, 1 - c))

    def to_hi(value):
        return send(value, lambda s, h, c: (s, 1 - h, c))

    def to_near(value):
        return send(value, lambda s, h, c: (s ^ 1, h, c))

    def to_cross(value):
        return send(value, lambda s, h, c: (s ^ 1, 1 - h, c))

    def to_owner(value):
        return send(value, lambda s, h, c: (s + 2 if s % 2 else s - 2, h, c))

    def to_strip(value):
        return send(value, lambda s, h, c: (s - 2 if s % 2 else s + 2, h, c))

    packed = jnp.stack([row_offset, col_offset, jnp.broadcast_to(counts, (per_tile,))])
    before_1 = send(packed, lambda s, h, c: (s + 1, h, c))
    before_2 = send(packed, lambda s, h, c: (s + 2, h, c))
    odd_pairs = [
        pair
        for pair in permutation(scan_size, lambda s, h, c: (s + 2, h, c))
        if (pair[0] // 4) % 2
    ]
    smatrix, where, odd_row = lax.optimization_barrier((smatrix, where, odd_row))
    field, own_amp, sent_amp = rows_first(where[5:], smatrix, amplitude)
    moved_amp = lax.ppermute(sent_amp, AXES, odd_pairs)

    coef_rem, coef_rest, low, high, live = coefficients(
        where, packed, before_1, before_2, beam_freq, beam_amp, parts, window
    )
    unit = 2 * quarter
    part = strip_rows // 2
    tile_rows = 4 * unit
    coefs = (coef_rem, coef_rest)

    def joined(mine, got):
        return mine.astype(F32) + got.astype(F32)

    mine_rem, other_rem, mine_loc, other_loc, mine_mid, other_mid = forward_waves(
        coefs, field
    )
    got_rem = to_core(other_rem)
    rem_top = to_owner(joined(mine_rem[:part], got_rem[:part]).astype(BF16))
    end_got = to_hi(joined(mine_rem[part:, unit:], got_rem[part:, unit:]).astype(BF16))
    rem_end = joined(mine_rem[part:, :unit], got_rem[part:, :unit]) + end_got.astype(F32)
    rem_end = to_owner(rem_end.astype(BF16))
    got_mid = to_core(other_mid)
    near_mid = to_near(joined(mine_mid[:, :unit], got_mid[:, :unit]).astype(BF16))
    cross_mid = to_cross(joined(mine_mid[:, unit:], got_mid[:, unit:]).astype(BF16))
    got_loc = to_core(other_loc)
    loc_end_got = to_hi(joined(mine_loc[part:, unit:], got_loc[part:, unit:]).astype(BF16))

    far_rows = slice(tile_rows + unit, tile_rows + 2 * unit)
    y_index = jnp.arange(part, dtype=F32)[:, None, None]
    inside = jnp.logical_and(low[None, far_rows] <= y_index, y_index < high[None, far_rows])
    top_sent = jnp.where(
        inside,
        joined(mine_loc[:part, unit:], got_loc[:part, unit:]),
        rem_top[:, unit:].astype(F32),
    )
    top_got = to_hi(top_sent.astype(BF16))

    tables = jnp.asarray(dft_matrices(window))
    ga_top, ga_end, grad_a, grad_b = far_gradient(
        tables, own_amp, moved_amp, odd_row, live,
        low, high, (mine_loc, got_loc, rem_top, top_got, loc_end_got, rem_end, near_mid, cross_mid),
    )

    ga_top_hi = to_hi(ga_top)
    rem_top = to_strip(ga_top)
    rem_end = to_strip(ga_end)
    other_a = to_core(grad_a)
    near, cross = to_near(grad_b), to_cross(grad_b)
    ga_end, ga_top_hi = lax.optimization_barrier((ga_end, ga_top_hi))
    rem_top_hi = to_strip(ga_top_hi)
    ga_end_hi = to_hi(ga_end)
    rem_end_hi = to_strip(ga_end_hi)
    middle = [near, cross, to_core(near), to_core(cross)]

    def ordered_pieces(rem, rem_hi, loc_hi):
        remote = [rem, rem_hi, to_core(rem), to_core(rem_hi)]
        return remote + [grad_a, loc_hi, other_a, to_core(loc_hi)] + middle

    out, done = backward_gradient(
        coefs, low, high, ordered_pieces(rem_top, rem_top_hi, ga_top_hi),
        parts, beams, 0, strip_rows, None,
    )
    rem_end_hi, done = lax.optimization_barrier((rem_end_hi, done))
    out, _ = backward_gradient(
        coefs, low, high, ordered_pieces(rem_end, rem_end_hi, ga_end_hi),
        parts, beams, part, strip_rows, (out, done),
    )
    return out


def solution(mesh):
    return jax.shard_map(
        body,
        mesh=mesh,
        in_specs=(
            P(None, "beam", "scan", None),
            P(None, "beam"),
            P(None, "beam"),
            P("scan"),
            P("scan"),
            P("scan"),
            P("scan", None, None),
        ),
        out_specs=P(None, "beam", "scan", None),
        check_vma=False,
    )
```

```python
import math

import jax
import jax.numpy as jnp
import ml_dtypes
import numpy as np
from jax import lax
from jax.experimental import pallas as pl
from jax.experimental.pallas import tpu as pltpu
from jax.sharding import PartitionSpec as P

TWO_PI = 6.283185307179586
ETA = 0.1
BF16 = jnp.bfloat16
F32 = jnp.float32
AXES = ("scan", "beam")
Y_BLOCK = 16


def permutation(scan_size, target):
    pairs = []
    for s in range(scan_size):
        for hi in range(2):
            for core in range(2):
                ts, th, tc = target(s, hi, core)
                pairs.append(((s * 2 + hi) * 2 + core, ((ts % scan_size) * 2 + th) * 2 + tc))
    return pairs


def coefficient_kernel(
    where_ref, here_ref, before_1_ref, before_2_ref, freq_ref, amp_ref,
    rem_ref, rest_ref, low_ref, high_ref, live_ref,
):
    me, odd, core, hi, tiles = (where_ref[k] for k in range(5))
    per_tile = here_ref.shape[1]
    quarter = per_tile // 4
    beams = freq_ref.shape[1]
    window = low_ref.shape[1]
    strip_rows = window // 2
    field_rows = tiles * strip_rows
    is_odd = odd == 1
    here, before_1, before_2 = here_ref[...], before_1_ref[...], before_2_ref[...]
    remote = jnp.where(is_odd, here, before_2)
    local = jnp.where(is_odd, before_2, here)
    back = 2 * odd
    parts = ((remote, me - 2 + back), (local, me - back), (before_1, me - 1))
    lane = lax.broadcasted_iota(jnp.int32, (quarter, per_tile), 1)
    index = lax.broadcasted_iota(jnp.int32, (quarter, per_tile), 0)
    step = 2 * quarter
    for part, (tile, tile_id) in enumerate(parts):
        for block in range(4):
            first = jnp.bitwise_xor(core, block // 2) * step + jnp.bitwise_xor(hi, block % 2) * quarter
            chosen = lane == first + index
            row = jnp.sum(jnp.where(chosen, tile[0:1], 0), axis=1, keepdims=True)
            col = jnp.sum(jnp.where(chosen, tile[1:2], 0), axis=1, keepdims=True)
            global_row = tile_id * strip_rows + row
            along_rows = jnp.bitwise_and(freq_ref[0:1] * global_row, field_rows - 1)
            along_cols = jnp.bitwise_and(freq_ref[1:2] * col, window - 1)
            turns = along_rows.astype(F32) / field_rows.astype(F32) + along_cols.astype(F32) / window
            angle = -TWO_PI * turns
            cos_part, sin_part = jnp.cos(angle), jnp.sin(angle)
            re = amp_ref[0:1] * cos_part - amp_ref[1:2] * sin_part
            im = amp_ref[0:1] * sin_part + amp_ref[1:2] * cos_part
            re, im = re.astype(BF16), im.astype(BF16)
            out_ref = rest_ref if part else rem_ref
            start = ((part - 1) * 4 if part else 0) * step + block * step
            out_ref[start : start + quarter, :beams] = re
            out_ref[start : start + quarter, beams:] = -im
            out_ref[start + quarter : start + step, :beams] = im
            out_ref[start + quarter : start + step, beams:] = re
            row = jnp.broadcast_to(row.astype(F32), (quarter, window))
            none, full = jnp.zeros_like(row), jnp.full_like(row, strip_rows)
            from_row = is_odd if part == 0 else jnp.logical_not(is_odd)
            if part == 2:
                low, high = none, full
            else:
                low, high = jnp.where(from_row, row, none), jnp.where(from_row, full, row)
            start = (part * 4 + block) * step
            for copy in range(2):
                at = start + copy * quarter
                low_ref[at : at + quarter] = low
                high_ref[at : at + quarter] = high
    first = core * step + hi * quarter
    position = lax.broadcasted_iota(jnp.int32, (quarter, window), 0) + first
    live_ref[...] = (position < local[2:3, :1]).astype(F32)


def coefficients(where, here, before_1, before_2, beam_freq, beam_amp, parts, window):
    beams = beam_freq.shape[1]
    per_tile = here.shape[1]
    shapes = [
        jax.ShapeDtypeStruct((2 * per_tile, parts * beams), BF16),
        jax.ShapeDtypeStruct((4 * per_tile, parts * beams), BF16),
        jax.ShapeDtypeStruct((6 * per_tile, window), F32),
        jax.ShapeDtypeStruct((6 * per_tile, window), F32),
        jax.ShapeDtypeStruct((per_tile // 4, window), F32),
    ]
    return pl.pallas_call(
        coefficient_kernel,
        in_specs=[pl.BlockSpec(memory_space=pltpu.SMEM)]
        + [pl.BlockSpec(memory_space=pltpu.VMEM)] * 5,
        out_specs=[pl.BlockSpec(memory_space=pltpu.VMEM)] * 5,
        out_shape=shapes,
        compiler_params=pltpu.CompilerParams(vmem_limit_bytes=16 << 20),
        name="coefficients",
    )(where, here, before_1, before_2, beam_freq, beam_amp)


def dft_matrices(window):
    counter = np.arange(window)
    angle = (counter[:, None] * counter[None, :] % window) * (2.0 * math.pi / window)
    re = np.cos(angle) / math.sqrt(window)
    im = -np.sin(angle) / math.sqrt(window)
    full = np.block([[re, im], [-im, re]])
    high = full.astype(ml_dtypes.bfloat16)
    low = (full - high.astype(np.float64)).astype(ml_dtypes.bfloat16)
    return np.stack([high, low, high.T, low.T])


def split(value):
    high = value.astype(BF16)
    return high, (value - high.astype(F32)).astype(BF16)


def dot(left, right):
    return jnp.dot(left, right, preferred_element_type=F32)


def right_product(value, high, low):
    value_hi, value_lo = split(value)
    return dot(value_hi, high) + (dot(value_lo, high) + dot(value_hi, low))


def left_product(high, low, value):
    value_hi, value_lo = split(value)
    return dot(high, value_hi) + (dot(high, value_lo) + dot(low, value_hi))


FIELD_CUTS = 4


def transpose_kernel(*refs):
    field_refs, out_ref = refs[:-1], refs[-1]
    _, beams, rows, window = field_refs[0].shape
    for k, field_ref in enumerate(field_refs):
        turned = jnp.swapaxes(field_ref[...].reshape(beams, rows, window), 0, 1)
        out_ref[:, k * beams : (k + 1) * beams, :] = turned


def rows_first(smatrix):
    parts, beams, strip_rows, window = smatrix.shape
    cut = beams // FIELD_CUTS
    return pl.pallas_call(
        transpose_kernel,
        grid=(strip_rows // Y_BLOCK, parts),
        in_specs=[
            pl.BlockSpec((1, cut, Y_BLOCK, window), lambda i, p, k=k: (p, k, i, 0))
            for k in range(FIELD_CUTS)
        ],
        out_specs=pl.BlockSpec((Y_BLOCK, beams, window), lambda i, p: (i, p, 0)),
        out_shape=jax.ShapeDtypeStruct((strip_rows, parts * beams, window), BF16),
        compiler_params=pltpu.CompilerParams(vmem_limit_bytes=38 << 20),
        cost_estimate=pl.CostEstimate(
            flops=0, bytes_accessed=4 * parts * beams * strip_rows * window, transcendentals=0
        ),
        name="rows_first",
    )(*[smatrix] * FIELD_CUTS)


def forward_kernel(rem_ref, rest_ref, field_ref, *out_refs):
    coef = jnp.concatenate([rem_ref[...], rest_ref[...]], axis=0)
    window = field_ref.shape[2]
    for y in range(0, field_ref.shape[0], 2):
        pair = jnp.concatenate([field_ref[y], field_ref[y + 1]], axis=1)
        waves = dot(coef, pair).astype(BF16)
        start = 0
        for out_ref in out_refs:
            rows = out_ref.shape[1]
            for k in range(2):
                out_ref[y + k] = waves[start : start + rows, k * window : (k + 1) * window]
            start += rows


def forward_waves(coefs, field):
    strip_rows, depth, window = field.shape
    total = sum(coef.shape[0] for coef in coefs)
    rows = total // 6
    block = Y_BLOCK // 2
    return pl.pallas_call(
        forward_kernel,
        grid=(strip_rows // block,),
        in_specs=[pl.BlockSpec(coef.shape, lambda i: (0, 0)) for coef in coefs]
        + [pl.BlockSpec((block, depth, window), lambda i: (i, 0, 0))],
        out_specs=[pl.BlockSpec((block, rows, window), lambda i: (i, 0, 0))] * 6,
        out_shape=[jax.ShapeDtypeStruct((strip_rows, rows, window), BF16)] * 6,
        compiler_params=pltpu.CompilerParams(vmem_limit_bytes=16 << 20),
        cost_estimate=pl.CostEstimate(
            flops=2 * total * depth * strip_rows * window,
            bytes_accessed=2 * (depth + total) * strip_rows * window,
            transcendentals=0,
        ),
        name="forward_waves",
    )(*coefs, field)


def backward_kernel(rem_ref, rest_ref, low_ref, high_ref, *refs):
    wave_refs, out_ref, turned = refs[:-2], refs[-2], refs[-1]
    parts, beams, _, window = out_ref.shape
    split_at = rem_ref.shape[0]

    @pl.when(pl.program_id(0) == 0)
    def turn():
        turned[:, :split_at] = rem_ref[...].T
        turned[:, split_at:] = rest_ref[...].T

    first = pl.program_id(0) * Y_BLOCK
    low, high = low_ref[...], high_ref[...]

    def masked(y):
        waves = jnp.concatenate([ref[y] for ref in wave_refs], axis=0)
        row = (first + y).astype(F32)
        keep = jnp.logical_and(low <= row, row < high)
        return jnp.where(keep, waves, jnp.zeros_like(waves))

    rows = []
    for y in range(0, Y_BLOCK, 2):
        waves = jnp.concatenate([masked(y), masked(y + 1)], axis=1)
        gradient = dot(turned[...], waves).astype(BF16)
        rows += [gradient[:, :window], gradient[:, window:]]
    by_row = jnp.stack(rows, axis=0)
    out_ref[...] = jnp.swapaxes(by_row, 0, 1).reshape(parts, beams, Y_BLOCK, window)


def backward_gradient(coefs, low, high, pieces, parts, beams):
    strip_rows, _, window = pieces[0].shape
    total = low.shape[0]

    def whole(value):
        return pl.BlockSpec(value.shape, lambda i: (0, 0))

    return pl.pallas_call(
        backward_kernel,
        grid=(strip_rows // Y_BLOCK,),
        in_specs=[whole(value) for value in (*coefs, low, high)]
        + [pl.BlockSpec((Y_BLOCK, *piece.shape[1:]), lambda i: (i, 0, 0)) for piece in pieces],
        out_specs=pl.BlockSpec((parts, beams, Y_BLOCK, window), lambda i: (0, 0, i, 0)),
        out_shape=jax.ShapeDtypeStruct((parts, beams, strip_rows, window), BF16),
        scratch_shapes=[pltpu.VMEM((parts * beams, total), BF16)],
        compiler_params=pltpu.CompilerParams(vmem_limit_bytes=32 << 20),
        cost_estimate=pl.CostEstimate(
            flops=2 * total * parts * beams * strip_rows * window,
            bytes_accessed=2 * (parts * beams + total) * strip_rows * window,
            transcendentals=0,
        ),
        name="backward_gradient",
    )(*coefs, low, high, *pieces)


def far_kernel(
    table_ref, amp_ref, moved_ref, odd_ref, live_ref, low_ref, high_ref, mine_ref, got_ref,
    rem_own_ref, a_got_ref, near_ref, cross_ref, ga_ref, gb_ref, mid, back,
):
    half, both, window = near_ref.shape
    count = both // 2
    fwd_hi, fwd_lo = table_ref[0], table_ref[1]
    inv_hi, inv_lo = table_ref[2], table_ref[3]
    own = mine_ref[...].astype(F32) + got_ref[...].astype(F32)
    row = lax.broadcasted_iota(jnp.int32, own.shape, 0).astype(F32)
    inside = jnp.logical_and(low_ref[...][None] <= row, row < high_ref[...][None])
    own = jnp.where(inside, own, rem_own_ref[...].astype(F32)) + a_got_ref[...].astype(F32)
    middle = near_ref[...].astype(F32) + cross_ref[...].astype(F32)
    for first, total in ((0, own), (half, middle)):
        rows = total.shape[0]
        pair = jnp.concatenate([total[:, :count], total[:, count:]], axis=2)
        out = right_product(pair.reshape(rows * count, 2 * window), fwd_hi, fwd_lo)
        out = jnp.swapaxes(out.reshape(rows, count, 2 * window), 0, 1)
        mid[:, first : first + rows, :] = out
    odd = jnp.broadcast_to(odd_ref[...], (2 * half, window)) > 0.0

    def amplitude(p):
        return jnp.where(odd, moved_ref[p].astype(F32), amp_ref[p].astype(F32))

    def one_pair(step, carry):
        first = step * 2
        stacked = []
        for p in range(2):
            rows = mid[first + p]
            stacked.append(jnp.concatenate([rows[:, :window], rows[:, window:]], axis=0))
        far = left_product(inv_hi, inv_lo, jnp.concatenate(stacked, axis=1))
        far_re, far_im = far[: 2 * half], far[2 * half :]
        measured = jnp.concatenate([amplitude(first), amplitude(first + 1)], axis=1)
        keep = 1.0 - measured * lax.rsqrt(far_re * far_re + far_im * far_im + ETA)
        residual = jnp.concatenate([far_re * keep, far_im * keep], axis=0)
        grad = left_product(fwd_hi, fwd_lo, residual)
        for p in range(2):
            lanes = slice(p * window, (p + 1) * window)
            pair = jnp.concatenate([grad[: 2 * half, lanes], grad[2 * half :, lanes]], axis=1)
            back[first + p] = pair
        return carry

    lax.fori_loop(0, count // 2, one_pair, 0, unroll=2)
    live = live_ref[...][:, None, :1]
    for first, g_ref in ((0, ga_ref), (half, gb_ref)):
        rows = back[:, first : first + half, :]
        out = right_product(rows.reshape(count * half, 2 * window), inv_hi, inv_lo)
        out = jnp.swapaxes(out.reshape(count, half, 2 * window) * live, 0, 1)
        g_ref[:, :count, :] = out[:, :, :window].astype(BF16)
        g_ref[:, count:, :] = out[:, :, window:].astype(BF16)


def far_gradient(tables, amplitude, moved, odd, live, low, high, pieces):
    half, both, window = pieces[-1].shape
    count = both // 2
    shape = jax.ShapeDtypeStruct((half, both, window), BF16)

    def whole(value):
        return pl.BlockSpec(value.shape, lambda i: (0,) * value.ndim)

    def rows_of(value, index):
        return pl.BlockSpec((*value.shape[:-2], both, window), lambda i: index)

    mine, got, *rest = pieces
    own_block = 4
    return pl.pallas_call(
        far_kernel,
        grid=(1,),
        in_specs=[whole(value) for value in (tables, amplitude, moved, odd, live)]
        + [rows_of(low, (own_block, 0)), rows_of(high, (own_block, 0))]
        + [rows_of(value, (0, 0, 0)) for value in (mine, got)]
        + [whole(value) for value in rest],
        out_specs=[whole(shape)] * 2,
        out_shape=[shape] * 2,
        scratch_shapes=[
            pltpu.VMEM((count, 2 * half, 2 * window), F32),
            pltpu.VMEM((count, 2 * half, 2 * window), F32),
        ],
        compiler_params=pltpu.CompilerParams(vmem_limit_bytes=36 << 20),
        cost_estimate=pl.CostEstimate(
            flops=12 * 2 * count * 2 * half * 4 * window * window,
            bytes_accessed=16 * half * both * window,
            transcendentals=count * window * window,
        ),
        name="far_gradient",
    )(tables, amplitude, moved, odd, live, low, high, *pieces)


def body(smatrix, beam_freq, beam_amp, row_offset, col_offset, counts, amplitude):
    parts, beams, strip_rows, window = smatrix.shape
    per_tile = row_offset.shape[0]
    quarter = per_tile // 4
    scan_size = lax.axis_size("scan")
    me = lax.axis_index("scan")
    beam_at = lax.axis_index("beam")
    hi, core = beam_at // 2, beam_at % 2
    at = core * 2 + hi
    odd = me % 2
    where = jnp.stack([me, odd, core, hi, jnp.int32(scan_size)]).astype(jnp.int32)
    odd_row = jnp.broadcast_to(odd.astype(F32), (1, window))

    def send(value, target):
        return lax.ppermute(value, AXES, permutation(scan_size, target))

    def to_core(value):
        return send(value, lambda s, h, c: (s, h, 1 - c))

    def to_hi(value):
        return send(value, lambda s, h, c: (s, 1 - h, c))

    def to_near(value):
        return send(value, lambda s, h, c: (s ^ 1, h, c))

    def to_cross(value):
        return send(value, lambda s, h, c: (s ^ 1, 1 - h, c))

    def to_owner(value):
        return send(value, lambda s, h, c: (s + 2 if s % 2 else s - 2, h, c))

    def to_strip(value):
        return send(value, lambda s, h, c: (s - 2 if s % 2 else s + 2, h, c))

    packed = jnp.stack([row_offset, col_offset, jnp.broadcast_to(counts, (per_tile,))])
    before_1 = send(packed, lambda s, h, c: (s + 1, h, c))
    before_2 = send(packed, lambda s, h, c: (s + 2, h, c))
    odd_pairs = [
        pair
        for pair in permutation(scan_size, lambda s, h, c: (s + 2, h, c))
        if (pair[0] // 4) % 2
    ]
    own_amp = lax.dynamic_slice_in_dim(amplitude, at * quarter, quarter, 0).astype(BF16)
    smatrix, where, odd_row, own_amp = lax.optimization_barrier((smatrix, where, odd_row, own_amp))
    moved_amp = lax.ppermute(own_amp, AXES, odd_pairs)
    field = rows_first(smatrix)

    coef_rem, coef_rest, low, high, live = coefficients(
        where, packed, before_1, before_2, beam_freq, beam_amp, parts, window
    )
    unit = 2 * quarter
    tile_rows = 4 * unit
    coefs = (coef_rem, coef_rest)

    def joined(mine, got):
        return mine.astype(F32) + got.astype(F32)

    mine_rem, other_rem, mine_loc, other_loc, mine_mid, other_mid = forward_waves(
        coefs, field
    )
    other_rem, moved_amp = lax.optimization_barrier((other_rem, moved_amp))
    got_rem = to_core(other_rem)
    rem_other = to_owner(joined(mine_rem[:, unit:], got_rem[:, unit:]).astype(BF16))
    got_mid = to_core(other_mid)
    near_mid = to_near(joined(mine_mid[:, :unit], got_mid[:, :unit]).astype(BF16))
    cross_mid = to_cross(joined(mine_mid[:, unit:], got_mid[:, unit:]).astype(BF16))
    got_loc = to_core(other_loc)
    rem_own = joined(mine_rem[:, :unit], got_rem[:, :unit]).astype(BF16)
    rem_own, rem_other = lax.optimization_barrier((rem_own, rem_other))
    rem_own = to_owner(rem_own)
    far_rows = slice(tile_rows + unit, tile_rows + 2 * unit)
    y_index = jnp.arange(strip_rows).astype(F32)[:, None, None]
    inside = jnp.logical_and(low[None, far_rows] <= y_index, y_index < high[None, far_rows])
    sent = jnp.where(inside, joined(mine_loc[:, unit:], got_loc[:, unit:]), rem_other.astype(F32))
    got_a = to_hi(sent.astype(BF16))

    tables = jnp.asarray(dft_matrices(window))
    grad_a, grad_b = far_gradient(
        tables, own_amp, moved_amp, odd_row, live,
        low, high, (mine_loc, got_loc, rem_own, got_a, near_mid, cross_mid),
    )

    a_hi = to_hi(grad_a)
    rem = to_strip(grad_a)
    grad_b, a_hi = lax.optimization_barrier((grad_b, a_hi))
    rem_hi = to_strip(a_hi)
    near, cross = to_near(grad_b), to_cross(grad_b)
    pieces = []
    for own, other in ((rem, rem_hi), (grad_a, a_hi), (near, cross)):
        pieces += [own, other, to_core(own), to_core(other)]
    return backward_gradient(coefs, low, high, pieces, parts, beams)


def solution(mesh):
    return jax.shard_map(
        body,
        mesh=mesh,
        in_specs=(
            P(None, "beam", "scan", None),
            P(None, "beam"),
            P(None, "beam"),
            P("scan"),
            P("scan"),
            P("scan"),
            P("scan", None, None),
        ),
        out_specs=P(None, "beam", "scan", None),
        check_vma=False,
    )
```

```python
import math

import jax
import jax.numpy as jnp
import ml_dtypes
import numpy as np
from jax import lax
from jax.experimental import pallas as pl
from jax.experimental.pallas import tpu as pltpu
from jax.sharding import PartitionSpec as P

TWO_PI = 6.283185307179586
ETA = 0.1
BF16 = jnp.bfloat16
F32 = jnp.float32
AXES = ("scan", "beam")
Y_BLOCK = 16


def permutation(scan_size, target):
    pairs = []
    for s in range(scan_size):
        for hi in range(2):
            for core in range(2):
                ts, th, tc = target(s, hi, core)
                pairs.append(((s * 2 + hi) * 2 + core, ((ts % scan_size) * 2 + th) * 2 + tc))
    return pairs


def coefficient_kernel(
    where_ref, here_ref, before_1_ref, before_2_ref, freq_ref, amp_ref,
    rem_ref, rest_ref, low_ref, high_ref, live_ref,
):
    me, odd, core, hi, tiles = (where_ref[k] for k in range(5))
    per_tile = here_ref.shape[1]
    quarter = per_tile // 4
    beams = freq_ref.shape[1]
    window = low_ref.shape[1]
    strip_rows = window // 2
    field_rows = tiles * strip_rows
    is_odd = odd == 1
    here, before_1, before_2 = here_ref[...], before_1_ref[...], before_2_ref[...]
    remote = jnp.where(is_odd, here, before_2)
    local = jnp.where(is_odd, before_2, here)
    back = 2 * odd
    parts = ((remote, me - 2 + back), (local, me - back), (before_1, me - 1))
    lane = lax.broadcasted_iota(jnp.int32, (quarter, per_tile), 1)
    index = lax.broadcasted_iota(jnp.int32, (quarter, per_tile), 0)
    step = 2 * quarter
    for part, (tile, tile_id) in enumerate(parts):
        for block in range(4):
            first = jnp.bitwise_xor(core, block // 2) * step + jnp.bitwise_xor(hi, block % 2) * quarter
            chosen = lane == first + index
            row = jnp.sum(jnp.where(chosen, tile[0:1], 0), axis=1, keepdims=True)
            col = jnp.sum(jnp.where(chosen, tile[1:2], 0), axis=1, keepdims=True)
            global_row = tile_id * strip_rows + row
            along_rows = jnp.bitwise_and(freq_ref[0:1] * global_row, field_rows - 1)
            along_cols = jnp.bitwise_and(freq_ref[1:2] * col, window - 1)
            turns = along_rows.astype(F32) / field_rows.astype(F32) + along_cols.astype(F32) / window
            angle = -TWO_PI * turns
            cos_part, sin_part = jnp.cos(angle), jnp.sin(angle)
            re = amp_ref[0:1] * cos_part - amp_ref[1:2] * sin_part
            im = amp_ref[0:1] * sin_part + amp_ref[1:2] * cos_part
            re, im = re.astype(BF16), im.astype(BF16)
            out_ref = rest_ref if part else rem_ref
            start = ((part - 1) * 4 if part else 0) * step + block * step
            out_ref[start : start + quarter, :beams] = re
            out_ref[start : start + quarter, beams:] = -im
            out_ref[start + quarter : start + step, :beams] = im
            out_ref[start + quarter : start + step, beams:] = re
            row = jnp.broadcast_to(row.astype(F32), (quarter, window))
            none, full = jnp.zeros_like(row), jnp.full_like(row, strip_rows)
            from_row = is_odd if part == 0 else jnp.logical_not(is_odd)
            if part == 2:
                low, high = none, full
            else:
                low, high = jnp.where(from_row, row, none), jnp.where(from_row, full, row)
            start = (part * 4 + block) * step
            for copy in range(2):
                at = start + copy * quarter
                low_ref[at : at + quarter] = low
                high_ref[at : at + quarter] = high
    first = core * step + hi * quarter
    position = lax.broadcasted_iota(jnp.int32, (quarter, window), 0) + first
    live_ref[...] = (position < local[2:3, :1]).astype(F32)


def coefficients(where, here, before_1, before_2, beam_freq, beam_amp, parts, window):
    beams = beam_freq.shape[1]
    per_tile = here.shape[1]
    shapes = [
        jax.ShapeDtypeStruct((2 * per_tile, parts * beams), BF16),
        jax.ShapeDtypeStruct((4 * per_tile, parts * beams), BF16),
        jax.ShapeDtypeStruct((6 * per_tile, window), F32),
        jax.ShapeDtypeStruct((6 * per_tile, window), F32),
        jax.ShapeDtypeStruct((per_tile // 4, window), F32),
    ]
    return pl.pallas_call(
        coefficient_kernel,
        in_specs=[pl.BlockSpec(memory_space=pltpu.SMEM)]
        + [pl.BlockSpec(memory_space=pltpu.VMEM)] * 5,
        out_specs=[pl.BlockSpec(memory_space=pltpu.VMEM)] * 5,
        out_shape=shapes,
        compiler_params=pltpu.CompilerParams(vmem_limit_bytes=16 << 20),
        name="coefficients",
    )(where, here, before_1, before_2, beam_freq, beam_amp)


def dft_matrices(window):
    counter = np.arange(window)
    angle = (counter[:, None] * counter[None, :] % window) * (2.0 * math.pi / window)
    re = np.cos(angle) / math.sqrt(window)
    im = -np.sin(angle) / math.sqrt(window)
    full = np.block([[re, im], [-im, re]])
    high = full.astype(ml_dtypes.bfloat16)
    low = (full - high.astype(np.float64)).astype(ml_dtypes.bfloat16)
    return np.stack([high, low, high.T, low.T])


def split(value):
    high = value.astype(BF16)
    return high, (value - high.astype(F32)).astype(BF16)


def dot(left, right):
    return jnp.dot(left, right, preferred_element_type=F32)


def right_product(value, high, low):
    value_hi, value_lo = split(value)
    return dot(value_hi, high) + (dot(value_lo, high) + dot(value_hi, low))


def right_rounded(value, high, low):
    value = value.astype(BF16)
    return dot(value, high) + dot(value, low)


def left_product(high, low, value):
    value_hi, value_lo = split(value)
    return dot(high, value_hi) + (dot(high, value_lo) + dot(low, value_hi))


FIELD_CUTS = 4


def transpose_kernel(*refs):
    field_refs, out_ref = refs[:-1], refs[-1]
    _, beams, rows, window = field_refs[0].shape
    for k, field_ref in enumerate(field_refs):
        turned = jnp.swapaxes(field_ref[...].reshape(beams, rows, window), 0, 1)
        out_ref[:, k * beams : (k + 1) * beams, :] = turned


def rows_first(smatrix):
    parts, beams, strip_rows, window = smatrix.shape
    cut = beams // FIELD_CUTS
    return pl.pallas_call(
        transpose_kernel,
        grid=(strip_rows // Y_BLOCK, parts),
        in_specs=[
            pl.BlockSpec((1, cut, Y_BLOCK, window), lambda i, p, k=k: (p, k, i, 0))
            for k in range(FIELD_CUTS)
        ],
        out_specs=pl.BlockSpec((Y_BLOCK, beams, window), lambda i, p: (i, p, 0)),
        out_shape=jax.ShapeDtypeStruct((strip_rows, parts * beams, window), BF16),
        compiler_params=pltpu.CompilerParams(vmem_limit_bytes=38 << 20),
        cost_estimate=pl.CostEstimate(
            flops=0, bytes_accessed=4 * parts * beams * strip_rows * window, transcendentals=0
        ),
        name="rows_first",
    )(*[smatrix] * FIELD_CUTS)


def forward_kernel(rem_ref, rest_ref, field_ref, *out_refs):
    coef = jnp.concatenate([rem_ref[...], rest_ref[...]], axis=0)
    window = field_ref.shape[2]
    for y in range(0, field_ref.shape[0], 2):
        pair = jnp.concatenate([field_ref[y], field_ref[y + 1]], axis=1)
        waves = dot(coef, pair).astype(BF16)
        start = 0
        for out_ref in out_refs:
            rows = out_ref.shape[1]
            for k in range(2):
                out_ref[y + k] = waves[start : start + rows, k * window : (k + 1) * window]
            start += rows


def forward_waves(coefs, field):
    strip_rows, depth, window = field.shape
    total = sum(coef.shape[0] for coef in coefs)
    rows = total // 6
    block = Y_BLOCK // 2
    return pl.pallas_call(
        forward_kernel,
        grid=(strip_rows // block,),
        in_specs=[pl.BlockSpec(coef.shape, lambda i: (0, 0)) for coef in coefs]
        + [pl.BlockSpec((block, depth, window), lambda i: (i, 0, 0))],
        out_specs=[pl.BlockSpec((block, rows, window), lambda i: (i, 0, 0))] * 6,
        out_shape=[jax.ShapeDtypeStruct((strip_rows, rows, window), BF16)] * 6,
        compiler_params=pltpu.CompilerParams(vmem_limit_bytes=16 << 20),
        cost_estimate=pl.CostEstimate(
            flops=2 * total * depth * strip_rows * window,
            bytes_accessed=2 * (depth + total) * strip_rows * window,
            transcendentals=0,
        ),
        name="forward_waves",
    )(*coefs, field)


def turn_kernel(rem_ref, rest_ref, out_ref):
    split_at = rem_ref.shape[0]
    out_ref[:, :split_at] = rem_ref[...].T
    out_ref[:, split_at:] = rest_ref[...].T


def turned(coefs):
    total, depth = sum(coef.shape[0] for coef in coefs), coefs[0].shape[1]
    return pl.pallas_call(
        turn_kernel,
        out_shape=jax.ShapeDtypeStruct((depth, total), BF16),
        compiler_params=pltpu.CompilerParams(vmem_limit_bytes=16 << 20),
        name="turned",
    )(*coefs)


def backward_kernel(coef_ref, low_ref, high_ref, *refs):
    wave_refs, out_ref = refs[:-1], refs[-1]
    parts, beams, _, window = out_ref.shape
    first = pl.program_id(0) * Y_BLOCK
    cut = low_ref.shape[0] // 3 * 2
    low, high = low_ref[:cut].astype(BF16), high_ref[:cut].astype(BF16)

    def masked(y):
        waves = jnp.concatenate([ref[y] for ref in wave_refs], axis=0)
        row = jnp.full((1, window), first + y, jnp.int32).astype(F32).astype(BF16)
        keep = jnp.logical_and(low <= row, row < high)
        edge = jnp.where(keep, waves[:cut], jnp.zeros_like(waves[:cut]))
        return jnp.concatenate([edge, waves[cut:]], axis=0)

    rows = []
    for y in range(0, Y_BLOCK, 2):
        waves = jnp.concatenate([masked(y), masked(y + 1)], axis=1)
        gradient = dot(coef_ref[...], waves).astype(BF16)
        rows += [gradient[:, :window], gradient[:, window:]]
    by_row = jnp.stack(rows, axis=0)
    out_ref[...] = jnp.swapaxes(by_row, 0, 1).reshape(parts, beams, Y_BLOCK, window)


def backward_gradient(coef_t, low, high, pieces, parts, beams):
    strip_rows, _, window = pieces[0].shape
    total = low.shape[0]

    def whole(value):
        return pl.BlockSpec(value.shape, lambda i: (0, 0))

    return pl.pallas_call(
        backward_kernel,
        grid=(strip_rows // Y_BLOCK,),
        in_specs=[whole(value) for value in (coef_t, low, high)]
        + [pl.BlockSpec((Y_BLOCK, *piece.shape[1:]), lambda i: (i, 0, 0)) for piece in pieces],
        out_specs=pl.BlockSpec((parts, beams, Y_BLOCK, window), lambda i: (0, 0, i, 0)),
        out_shape=jax.ShapeDtypeStruct((parts, beams, strip_rows, window), BF16),
        compiler_params=pltpu.CompilerParams(vmem_limit_bytes=32 << 20),
        cost_estimate=pl.CostEstimate(
            flops=2 * total * parts * beams * strip_rows * window,
            bytes_accessed=2 * (parts * beams + total) * strip_rows * window,
            transcendentals=0,
        ),
        name="backward_gradient",
    )(coef_t, low, high, *pieces)


def far_kernel(
    table_ref, amp_ref, moved_ref, odd_ref, live_ref, low_ref, high_ref, mine_ref, got_ref,
    rem_own_ref, a_got_ref, near_ref, cross_ref, ga_ref, gb_ref, mid, back,
):
    half, both, window = near_ref.shape
    count = both // 2
    fwd_hi, fwd_lo = table_ref[0], table_ref[1]
    inv_hi, inv_lo = table_ref[2], table_ref[3]
    own = mine_ref[...].astype(F32) + got_ref[...].astype(F32)
    row = lax.broadcasted_iota(jnp.int32, own.shape, 0).astype(F32)
    inside = jnp.logical_and(low_ref[...][None] <= row, row < high_ref[...][None])
    own = jnp.where(inside, own, rem_own_ref[...].astype(F32)) + a_got_ref[...].astype(F32)
    middle = near_ref[...].astype(F32) + cross_ref[...].astype(F32)
    for first, total in ((0, own), (half, middle)):
        rows = total.shape[0]
        pair = jnp.concatenate([total[:, :count], total[:, count:]], axis=2)
        out = right_product(pair.reshape(rows * count, 2 * window), fwd_hi, fwd_lo)
        out = jnp.swapaxes(out.reshape(rows, count, 2 * window), 0, 1)
        mid[:, first : first + rows, :] = out
    odd = jnp.broadcast_to(odd_ref[...], (2 * half, window)) > 0.0

    def amplitude(p):
        return jnp.where(odd, moved_ref[p].astype(F32), amp_ref[p].astype(F32))

    def one_pair(step, carry):
        first = step * 2
        stacked = []
        for p in range(2):
            rows = mid[first + p]
            stacked.append(jnp.concatenate([rows[:, :window], rows[:, window:]], axis=0))
        far = left_product(inv_hi, inv_lo, jnp.concatenate(stacked, axis=1))
        far_re, far_im = far[: 2 * half], far[2 * half :]
        measured = jnp.concatenate([amplitude(first), amplitude(first + 1)], axis=1)
        keep = 1.0 - measured * lax.rsqrt(far_re * far_re + far_im * far_im + ETA)
        residual = jnp.concatenate([far_re * keep, far_im * keep], axis=0)
        grad = left_product(fwd_hi, fwd_lo, residual)
        for p in range(2):
            lanes = slice(p * window, (p + 1) * window)
            pair = jnp.concatenate([grad[: 2 * half, lanes], grad[2 * half :, lanes]], axis=1)
            back[first + p] = pair
        return carry

    lax.fori_loop(0, count // 2, one_pair, 0, unroll=2)
    live = live_ref[...][:, None, :1]
    for first, g_ref in ((0, ga_ref), (half, gb_ref)):
        rows = back[:, first : first + half, :]
        out = right_rounded(rows.reshape(count * half, 2 * window), inv_hi, inv_lo)
        out = jnp.swapaxes(out.reshape(count, half, 2 * window) * live, 0, 1)
        g_ref[:, :count, :] = out[:, :, :window].astype(BF16)
        g_ref[:, count:, :] = out[:, :, window:].astype(BF16)


def far_gradient(tables, amplitude, moved, odd, live, low, high, pieces):
    half, both, window = pieces[-1].shape
    count = both // 2
    shape = jax.ShapeDtypeStruct((half, both, window), BF16)

    def whole(value):
        return pl.BlockSpec(value.shape, lambda i: (0,) * value.ndim)

    def rows_of(value, index):
        return pl.BlockSpec((*value.shape[:-2], both, window), lambda i: index)

    mine, got, *rest = pieces
    own_block = 4
    return pl.pallas_call(
        far_kernel,
        grid=(1,),
        in_specs=[whole(value) for value in (tables, amplitude, moved, odd, live)]
        + [rows_of(low, (own_block, 0)), rows_of(high, (own_block, 0))]
        + [rows_of(value, (0, 0, 0)) for value in (mine, got)]
        + [whole(value) for value in rest],
        out_specs=[whole(shape)] * 2,
        out_shape=[shape] * 2,
        scratch_shapes=[
            pltpu.VMEM((count, 2 * half, 2 * window), F32),
            pltpu.VMEM((count, 2 * half, 2 * window), F32),
        ],
        compiler_params=pltpu.CompilerParams(vmem_limit_bytes=36 << 20),
        cost_estimate=pl.CostEstimate(
            flops=12 * 2 * count * 2 * half * 4 * window * window,
            bytes_accessed=16 * half * both * window,
            transcendentals=count * window * window,
        ),
        name="far_gradient",
    )(tables, amplitude, moved, odd, live, low, high, *pieces)


def body(smatrix, beam_freq, beam_amp, row_offset, col_offset, counts, amplitude):
    parts, beams, strip_rows, window = smatrix.shape
    per_tile = row_offset.shape[0]
    quarter = per_tile // 4
    scan_size = lax.axis_size("scan")
    me = lax.axis_index("scan")
    beam_at = lax.axis_index("beam")
    hi, core = beam_at // 2, beam_at % 2
    at = core * 2 + hi
    odd = me % 2
    where = jnp.stack([me, odd, core, hi, jnp.int32(scan_size)]).astype(jnp.int32)
    odd_row = jnp.broadcast_to(odd.astype(F32), (1, window))

    def send(value, target):
        return lax.ppermute(value, AXES, permutation(scan_size, target))

    def to_core(value):
        return send(value, lambda s, h, c: (s, h, 1 - c))

    def to_hi(value):
        return send(value, lambda s, h, c: (s, 1 - h, c))

    def to_near(value):
        return send(value, lambda s, h, c: (s ^ 1, h, c))

    def to_cross(value):
        return send(value, lambda s, h, c: (s ^ 1, 1 - h, c))

    def to_owner(value):
        return send(value, lambda s, h, c: (s + 2 if s % 2 else s - 2, h, c))

    def to_strip(value):
        return send(value, lambda s, h, c: (s - 2 if s % 2 else s + 2, h, c))

    packed = jnp.stack([row_offset, col_offset, jnp.broadcast_to(counts, (per_tile,))])
    before_1 = send(packed, lambda s, h, c: (s + 1, h, c))
    before_2 = send(packed, lambda s, h, c: (s + 2, h, c))
    odd_pairs = [
        pair
        for pair in permutation(scan_size, lambda s, h, c: (s + 2, h, c))
        if (pair[0] // 4) % 2
    ]
    own_amp = lax.dynamic_slice_in_dim(amplitude, at * quarter, quarter, 0).astype(BF16)
    smatrix, where, odd_row, own_amp = lax.optimization_barrier((smatrix, where, odd_row, own_amp))
    moved_amp = lax.ppermute(own_amp, AXES, odd_pairs)
    field = rows_first(smatrix)

    coef_rem, coef_rest, low, high, live = coefficients(
        where, packed, before_1, before_2, beam_freq, beam_amp, parts, window
    )
    unit = 2 * quarter
    tile_rows = 4 * unit
    coefs = (coef_rem, coef_rest)

    def joined(mine, got):
        return mine.astype(F32) + got.astype(F32)

    mine_rem, other_rem, mine_loc, other_loc, mine_mid, other_mid = forward_waves(
        coefs, field
    )
    other_rem, moved_amp = lax.optimization_barrier((other_rem, moved_amp))
    got_rem = to_core(other_rem)
    rem_other = to_owner(joined(mine_rem[:, unit:], got_rem[:, unit:]).astype(BF16))
    got_mid = to_core(other_mid)
    near_mid = to_near(joined(mine_mid[:, :unit], got_mid[:, :unit]).astype(BF16))
    cross_mid = to_cross(joined(mine_mid[:, unit:], got_mid[:, unit:]).astype(BF16))
    got_loc = to_core(other_loc)
    rem_own = joined(mine_rem[:, :unit], got_rem[:, :unit]).astype(BF16)
    rem_own, rem_other = lax.optimization_barrier((rem_own, rem_other))
    rem_own = to_owner(rem_own)
    far_rows = slice(tile_rows + unit, tile_rows + 2 * unit)
    y_index = jnp.arange(strip_rows).astype(F32)[:, None, None]
    inside = jnp.logical_and(low[None, far_rows] <= y_index, y_index < high[None, far_rows])
    sent = jnp.where(inside, joined(mine_loc[:, unit:], got_loc[:, unit:]), rem_other.astype(F32))
    got_a = to_hi(sent.astype(BF16))
    coef_t = turned(coefs)

    tables = jnp.asarray(dft_matrices(window))
    grad_a, grad_b = far_gradient(
        tables, own_amp, moved_amp, odd_row, live,
        low, high, (mine_loc, got_loc, rem_own, got_a, near_mid, cross_mid),
    )

    a_hi = to_hi(grad_a)
    rem = to_strip(grad_a)
    rem_hi = to_strip(a_hi)
    near, cross = to_near(grad_b), to_cross(grad_b)
    pieces = []
    for own, other in ((rem, rem_hi), (grad_a, a_hi), (near, cross)):
        pieces += [own, other, to_core(own), to_core(other)]
    return backward_gradient(coef_t, low, high, pieces, parts, beams)


def solution(mesh):
    return jax.shard_map(
        body,
        mesh=mesh,
        in_specs=(
            P(None, "beam", "scan", None),
            P(None, "beam"),
            P(None, "beam"),
            P("scan"),
            P("scan"),
            P("scan"),
            P("scan", None, None),
        ),
        out_specs=P(None, "beam", "scan", None),
        check_vma=False,
    )
```

```python
import math

import jax
import jax.numpy as jnp
import ml_dtypes
import numpy as np
from jax import lax
from jax.experimental import pallas as pl
from jax.experimental.pallas import tpu as pltpu
from jax.sharding import PartitionSpec as P

TWO_PI = 6.283185307179586
ETA = 0.1
BF16 = jnp.bfloat16
F32 = jnp.float32
AXES = ("scan", "beam")
Y_BLOCK = 16


def permutation(scan_size, target):
    pairs = []
    for s in range(scan_size):
        for hi in range(2):
            for core in range(2):
                ts, th, tc = target(s, hi, core)
                pairs.append(((s * 2 + hi) * 2 + core, ((ts % scan_size) * 2 + th) * 2 + tc))
    return pairs


def coefficient_kernel(
    where_ref, here_ref, before_1_ref, before_2_ref, freq_ref, amp_ref,
    rem_ref, rest_ref, low_ref, high_ref, live_ref,
):
    me, odd, core, hi, tiles = (where_ref[k] for k in range(5))
    per_tile = here_ref.shape[1]
    quarter = per_tile // 4
    beams = freq_ref.shape[1]
    window = low_ref.shape[1]
    strip_rows = window // 2
    field_rows = tiles * strip_rows
    is_odd = odd == 1
    here, before_1, before_2 = here_ref[...], before_1_ref[...], before_2_ref[...]
    remote = jnp.where(is_odd, here, before_2)
    local = jnp.where(is_odd, before_2, here)
    back = 2 * odd
    parts = ((remote, me - 2 + back), (local, me - back), (before_1, me - 1))
    lane = lax.broadcasted_iota(jnp.int32, (quarter, per_tile), 1)
    index = lax.broadcasted_iota(jnp.int32, (quarter, per_tile), 0)
    step = 2 * quarter
    for part, (tile, tile_id) in enumerate(parts):
        for block in range(4):
            first = jnp.bitwise_xor(core, block // 2) * step + jnp.bitwise_xor(hi, block % 2) * quarter
            chosen = lane == first + index
            row = jnp.sum(jnp.where(chosen, tile[0:1], 0), axis=1, keepdims=True)
            col = jnp.sum(jnp.where(chosen, tile[1:2], 0), axis=1, keepdims=True)
            global_row = tile_id * strip_rows + row
            along_rows = jnp.bitwise_and(freq_ref[0:1] * global_row, field_rows - 1)
            along_cols = jnp.bitwise_and(freq_ref[1:2] * col, window - 1)
            turns = along_rows.astype(F32) / field_rows.astype(F32) + along_cols.astype(F32) / window
            angle = -TWO_PI * turns
            cos_part, sin_part = jnp.cos(angle), jnp.sin(angle)
            re = amp_ref[0:1] * cos_part - amp_ref[1:2] * sin_part
            im = amp_ref[0:1] * sin_part + amp_ref[1:2] * cos_part
            re, im = re.astype(BF16), im.astype(BF16)
            out_ref = rest_ref if part else rem_ref
            start = ((part - 1) * 4 if part else 0) * step + block * step
            out_ref[start : start + quarter, :beams] = re
            out_ref[start : start + quarter, beams:] = -im
            out_ref[start + quarter : start + step, :beams] = im
            out_ref[start + quarter : start + step, beams:] = re
            row = jnp.broadcast_to(row.astype(F32), (quarter, window))
            none, full = jnp.zeros_like(row), jnp.full_like(row, strip_rows)
            from_row = is_odd if part == 0 else jnp.logical_not(is_odd)
            if part == 2:
                low, high = none, full
            else:
                low, high = jnp.where(from_row, row, none), jnp.where(from_row, full, row)
            start = (part * 4 + block) * step
            for copy in range(2):
                at = start + copy * quarter
                low_ref[at : at + quarter] = low
                high_ref[at : at + quarter] = high
    first = core * step + hi * quarter
    position = lax.broadcasted_iota(jnp.int32, (quarter, window), 0) + first
    live_ref[...] = (position < local[2:3, :1]).astype(F32)


def coefficients(where, here, before_1, before_2, beam_freq, beam_amp, parts, window):
    beams = beam_freq.shape[1]
    per_tile = here.shape[1]
    shapes = [
        jax.ShapeDtypeStruct((2 * per_tile, parts * beams), BF16),
        jax.ShapeDtypeStruct((4 * per_tile, parts * beams), BF16),
        jax.ShapeDtypeStruct((6 * per_tile, window), F32),
        jax.ShapeDtypeStruct((6 * per_tile, window), F32),
        jax.ShapeDtypeStruct((per_tile // 4, window), F32),
    ]
    return pl.pallas_call(
        coefficient_kernel,
        in_specs=[pl.BlockSpec(memory_space=pltpu.SMEM)]
        + [pl.BlockSpec(memory_space=pltpu.VMEM)] * 5,
        out_specs=[pl.BlockSpec(memory_space=pltpu.VMEM)] * 5,
        out_shape=shapes,
        compiler_params=pltpu.CompilerParams(vmem_limit_bytes=16 << 20),
        name="coefficients",
    )(where, here, before_1, before_2, beam_freq, beam_amp)


def dft_matrices(window):
    counter = np.arange(window)
    angle = (counter[:, None] * counter[None, :] % window) * (2.0 * math.pi / window)
    re = np.cos(angle) / math.sqrt(window)
    im = -np.sin(angle) / math.sqrt(window)
    full = np.block([[re, im], [-im, re]])
    high = full.astype(ml_dtypes.bfloat16)
    low = (full - high.astype(np.float64)).astype(ml_dtypes.bfloat16)
    return np.stack([high, low, high.T, low.T])


def split(value):
    high = value.astype(BF16)
    return high, (value - high.astype(F32)).astype(BF16)


def dot(left, right):
    return jnp.dot(left, right, preferred_element_type=F32)


def right_product(value, high, low):
    value_hi, value_lo = split(value)
    return dot(value_hi, high) + (dot(value_lo, high) + dot(value_hi, low))


def right_rounded(value, high, low):
    value = value.astype(BF16)
    return dot(value, high) + dot(value, low)


def left_product(high, low, value):
    value_hi, value_lo = split(value)
    return dot(high, value_hi) + (dot(high, value_lo) + dot(low, value_hi))


FIELD_CUTS = 4


def transpose_kernel(*refs):
    field_refs, out_ref = refs[:-1], refs[-1]
    _, beams, rows, window = field_refs[0].shape
    for k, field_ref in enumerate(field_refs):
        turned = jnp.swapaxes(field_ref[...].reshape(beams, rows, window), 0, 1)
        out_ref[:, k * beams : (k + 1) * beams, :] = turned


def rows_first(smatrix):
    parts, beams, strip_rows, window = smatrix.shape
    cut = beams // FIELD_CUTS
    return pl.pallas_call(
        transpose_kernel,
        grid=(strip_rows // Y_BLOCK, parts),
        in_specs=[
            pl.BlockSpec((1, cut, Y_BLOCK, window), lambda i, p, k=k: (p, k, i, 0))
            for k in range(FIELD_CUTS)
        ],
        out_specs=pl.BlockSpec((Y_BLOCK, beams, window), lambda i, p: (i, p, 0)),
        out_shape=jax.ShapeDtypeStruct((strip_rows, parts * beams, window), BF16),
        compiler_params=pltpu.CompilerParams(vmem_limit_bytes=38 << 20),
        cost_estimate=pl.CostEstimate(
            flops=0, bytes_accessed=4 * parts * beams * strip_rows * window, transcendentals=0
        ),
        name="rows_first",
    )(*[smatrix] * FIELD_CUTS)


def forward_kernel(rem_ref, rest_ref, field_ref, *out_refs):
    coef = jnp.concatenate([rem_ref[...], rest_ref[...]], axis=0)
    window = field_ref.shape[2]
    for y in range(0, field_ref.shape[0], 2):
        pair = jnp.concatenate([field_ref[y], field_ref[y + 1]], axis=1)
        waves = dot(coef, pair).astype(BF16)
        start = 0
        for out_ref in out_refs:
            rows = out_ref.shape[1]
            for k in range(2):
                out_ref[y + k] = waves[start : start + rows, k * window : (k + 1) * window]
            start += rows


def forward_waves(coefs, field):
    strip_rows, depth, window = field.shape
    total = sum(coef.shape[0] for coef in coefs)
    rows = total // 6
    block = Y_BLOCK // 2
    return pl.pallas_call(
        forward_kernel,
        grid=(strip_rows // block,),
        in_specs=[pl.BlockSpec(coef.shape, lambda i: (0, 0)) for coef in coefs]
        + [pl.BlockSpec((block, depth, window), lambda i: (i, 0, 0))],
        out_specs=[pl.BlockSpec((block, rows, window), lambda i: (i, 0, 0))] * 6,
        out_shape=[jax.ShapeDtypeStruct((strip_rows, rows, window), BF16)] * 6,
        compiler_params=pltpu.CompilerParams(vmem_limit_bytes=16 << 20),
        cost_estimate=pl.CostEstimate(
            flops=2 * total * depth * strip_rows * window,
            bytes_accessed=2 * (depth + total) * strip_rows * window,
            transcendentals=0,
        ),
        name="forward_waves",
    )(*coefs, field)


def turn_kernel(rem_ref, rest_ref, out_ref):
    split_at = rem_ref.shape[0]
    out_ref[:, :split_at] = rem_ref[...].T
    out_ref[:, split_at:] = rest_ref[...].T


def turned(coefs):
    total, depth = sum(coef.shape[0] for coef in coefs), coefs[0].shape[1]
    return pl.pallas_call(
        turn_kernel,
        out_shape=jax.ShapeDtypeStruct((depth, total), BF16),
        compiler_params=pltpu.CompilerParams(vmem_limit_bytes=16 << 20),
        name="turned",
    )(*coefs)


def backward_kernel(coef_ref, low_ref, high_ref, *refs):
    wave_refs, out_ref = refs[:-1], refs[-1]
    parts, beams, _, window = out_ref.shape
    first = pl.program_id(0) * Y_BLOCK
    cut = low_ref.shape[0] // 3 * 2
    low, high = low_ref[:cut].astype(BF16), high_ref[:cut].astype(BF16)

    def masked(y):
        waves = jnp.concatenate([ref[y] for ref in wave_refs], axis=0)
        row = jnp.full((1, window), first + y, jnp.int32).astype(F32).astype(BF16)
        keep = jnp.logical_and(low <= row, row < high)
        edge = jnp.where(keep, waves[:cut], jnp.zeros_like(waves[:cut]))
        return jnp.concatenate([edge, waves[cut:]], axis=0)

    rows = []
    for y in range(0, Y_BLOCK, 2):
        waves = jnp.concatenate([masked(y), masked(y + 1)], axis=1)
        gradient = dot(coef_ref[...], waves).astype(BF16)
        rows += [gradient[:, :window], gradient[:, window:]]
    by_row = jnp.stack(rows, axis=0)
    out_ref[...] = jnp.swapaxes(by_row, 0, 1).reshape(parts, beams, Y_BLOCK, window)


def backward_gradient(coef_t, low, high, pieces, parts, beams):
    strip_rows, _, window = pieces[0].shape
    total = low.shape[0]

    def whole(value):
        return pl.BlockSpec(value.shape, lambda i: (0, 0))

    return pl.pallas_call(
        backward_kernel,
        grid=(strip_rows // Y_BLOCK,),
        in_specs=[whole(value) for value in (coef_t, low, high)]
        + [pl.BlockSpec((Y_BLOCK, *piece.shape[1:]), lambda i: (i, 0, 0)) for piece in pieces],
        out_specs=pl.BlockSpec((parts, beams, Y_BLOCK, window), lambda i: (0, 0, i, 0)),
        out_shape=jax.ShapeDtypeStruct((parts, beams, strip_rows, window), BF16),
        compiler_params=pltpu.CompilerParams(vmem_limit_bytes=32 << 20),
        cost_estimate=pl.CostEstimate(
            flops=2 * total * parts * beams * strip_rows * window,
            bytes_accessed=2 * (parts * beams + total) * strip_rows * window,
            transcendentals=0,
        ),
        name="backward_gradient",
    )(coef_t, low, high, *pieces)


def far_kernel(
    table_ref, amp_ref, moved_ref, odd_ref, live_ref, low_ref, high_ref, mine_ref, got_ref,
    rem_own_ref, top_got_ref, end_got_ref, near_ref, cross_ref, ga_ref, gb_ref, mid, back,
):
    half, both, window = near_ref.shape
    count = both // 2
    fwd_hi, fwd_lo = table_ref[0], table_ref[1]
    inv_hi, inv_lo = table_ref[2], table_ref[3]
    own = mine_ref[...].astype(F32) + got_ref[...].astype(F32)
    row = lax.broadcasted_iota(jnp.int32, own.shape, 0).astype(F32)
    inside = jnp.logical_and(low_ref[...][None] <= row, row < high_ref[...][None])
    got_a = jnp.concatenate([top_got_ref[...], end_got_ref[...]], axis=0)
    own = jnp.where(inside, own, rem_own_ref[...].astype(F32)) + got_a.astype(F32)
    middle = near_ref[...].astype(F32) + cross_ref[...].astype(F32)
    for first, total in ((0, own), (half, middle)):
        rows = total.shape[0]
        pair = jnp.concatenate([total[:, :count], total[:, count:]], axis=2)
        out = right_product(pair.reshape(rows * count, 2 * window), fwd_hi, fwd_lo)
        out = jnp.swapaxes(out.reshape(rows, count, 2 * window), 0, 1)
        mid[:, first : first + rows, :] = out
    odd = jnp.broadcast_to(odd_ref[...], (2 * half, window)) > 0.0

    def amplitude(p):
        return jnp.where(odd, moved_ref[p].astype(F32), amp_ref[p].astype(F32))

    def one_pair(step, carry):
        first = step * 2
        stacked = []
        for p in range(2):
            rows = mid[first + p]
            stacked.append(jnp.concatenate([rows[:, :window], rows[:, window:]], axis=0))
        far = left_product(inv_hi, inv_lo, jnp.concatenate(stacked, axis=1))
        far_re, far_im = far[: 2 * half], far[2 * half :]
        measured = jnp.concatenate([amplitude(first), amplitude(first + 1)], axis=1)
        keep = 1.0 - measured * lax.rsqrt(far_re * far_re + far_im * far_im + ETA)
        residual = jnp.concatenate([far_re * keep, far_im * keep], axis=0)
        grad = left_product(fwd_hi, fwd_lo, residual)
        for p in range(2):
            lanes = slice(p * window, (p + 1) * window)
            pair = jnp.concatenate([grad[: 2 * half, lanes], grad[2 * half :, lanes]], axis=1)
            back[first + p] = pair
        return carry

    lax.fori_loop(0, count // 2, one_pair, 0, unroll=8)
    live = live_ref[...][:, None, :1]
    for first, g_ref in ((0, ga_ref), (half, gb_ref)):
        rows = back[:, first : first + half, :]
        out = right_rounded(rows.reshape(count * half, 2 * window), inv_hi, inv_lo)
        out = jnp.swapaxes(out.reshape(count, half, 2 * window) * live, 0, 1)
        g_ref[:, :count, :] = out[:, :, :window].astype(BF16)
        g_ref[:, count:, :] = out[:, :, window:].astype(BF16)


def far_gradient(tables, amplitude, moved, odd, live, low, high, pieces):
    half, both, window = pieces[-1].shape
    count = both // 2
    shape = jax.ShapeDtypeStruct((half, both, window), BF16)

    def whole(value):
        return pl.BlockSpec(value.shape, lambda i: (0,) * value.ndim)

    def rows_of(value, index):
        return pl.BlockSpec((*value.shape[:-2], both, window), lambda i: index)

    mine, got, *rest = pieces
    own_block = 4
    return pl.pallas_call(
        far_kernel,
        grid=(1,),
        in_specs=[whole(value) for value in (tables, amplitude, moved, odd, live)]
        + [rows_of(low, (own_block, 0)), rows_of(high, (own_block, 0))]
        + [rows_of(value, (0, 0, 0)) for value in (mine, got)]
        + [whole(value) for value in rest],
        out_specs=[whole(shape)] * 2,
        out_shape=[shape] * 2,
        scratch_shapes=[
            pltpu.VMEM((count, 2 * half, 2 * window), F32),
            pltpu.VMEM((count, 2 * half, 2 * window), F32),
        ],
        compiler_params=pltpu.CompilerParams(vmem_limit_bytes=36 << 20),
        cost_estimate=pl.CostEstimate(
            flops=12 * 2 * count * 2 * half * 4 * window * window,
            bytes_accessed=16 * half * both * window,
            transcendentals=count * window * window,
        ),
        name="far_gradient",
    )(tables, amplitude, moved, odd, live, low, high, *pieces)


def body(smatrix, beam_freq, beam_amp, row_offset, col_offset, counts, amplitude):
    parts, beams, strip_rows, window = smatrix.shape
    per_tile = row_offset.shape[0]
    quarter = per_tile // 4
    scan_size = lax.axis_size("scan")
    me = lax.axis_index("scan")
    beam_at = lax.axis_index("beam")
    hi, core = beam_at // 2, beam_at % 2
    at = core * 2 + hi
    odd = me % 2
    where = jnp.stack([me, odd, core, hi, jnp.int32(scan_size)]).astype(jnp.int32)
    odd_row = jnp.broadcast_to(odd.astype(F32), (1, window))

    def send(value, target):
        return lax.ppermute(value, AXES, permutation(scan_size, target))

    def to_core(value):
        return send(value, lambda s, h, c: (s, h, 1 - c))

    def to_hi(value):
        return send(value, lambda s, h, c: (s, 1 - h, c))

    def to_near(value):
        return send(value, lambda s, h, c: (s ^ 1, h, c))

    def to_cross(value):
        return send(value, lambda s, h, c: (s ^ 1, 1 - h, c))

    def to_owner(value):
        return send(value, lambda s, h, c: (s + 2 if s % 2 else s - 2, h, c))

    def to_strip(value):
        return send(value, lambda s, h, c: (s - 2 if s % 2 else s + 2, h, c))

    packed = jnp.stack([row_offset, col_offset, jnp.broadcast_to(counts, (per_tile,))])
    before_1 = send(packed, lambda s, h, c: (s + 1, h, c))
    before_2 = send(packed, lambda s, h, c: (s + 2, h, c))
    odd_pairs = [
        pair
        for pair in permutation(scan_size, lambda s, h, c: (s + 2, h, c))
        if (pair[0] // 4) % 2
    ]
    own_amp = lax.dynamic_slice_in_dim(amplitude, at * quarter, quarter, 0).astype(BF16)
    smatrix, where, odd_row, own_amp = lax.optimization_barrier((smatrix, where, odd_row, own_amp))
    moved_amp = lax.ppermute(own_amp, AXES, odd_pairs)
    field = rows_first(smatrix)

    coef_rem, coef_rest, low, high, live = coefficients(
        where, packed, before_1, before_2, beam_freq, beam_amp, parts, window
    )
    unit = 2 * quarter
    tile_rows = 4 * unit
    coefs = (coef_rem, coef_rest)

    def joined(mine, got):
        return mine.astype(F32) + got.astype(F32)

    mine_rem, other_rem, mine_loc, other_loc, mine_mid, other_mid = forward_waves(
        coefs, field
    )
    other_rem, moved_amp = lax.optimization_barrier((other_rem, moved_amp))
    got_rem = to_core(other_rem)
    part = strip_rows // 2
    halves = (slice(0, part), slice(part, strip_rows))
    rem_other = [
        to_owner(joined(mine_rem[half, unit:], got_rem[half, unit:]).astype(BF16)) for half in halves
    ]
    got_mid = to_core(other_mid)
    near_mid = to_near(joined(mine_mid[:, :unit], got_mid[:, :unit]).astype(BF16))
    cross_mid = to_cross(joined(mine_mid[:, unit:], got_mid[:, unit:]).astype(BF16))
    got_loc = to_core(other_loc)
    rem_own = joined(mine_rem[:, :unit], got_rem[:, :unit]).astype(BF16)
    rem_own, rem_other[1] = lax.optimization_barrier((rem_own, rem_other[1]))
    rem_own = to_owner(rem_own)
    far_rows = slice(tile_rows + unit, tile_rows + 2 * unit)
    local = got_loc
    got_a = []
    for half, rem_half in zip(halves, rem_other):
        if got_a:
            local, got_a[0] = lax.optimization_barrier((local, got_a[0]))
        y_index = jnp.arange(half.start, half.stop).astype(F32)[:, None, None]
        inside = jnp.logical_and(low[None, far_rows] <= y_index, y_index < high[None, far_rows])
        sent = jnp.where(
            inside, joined(mine_loc[half, unit:], local[half, unit:]), rem_half.astype(F32)
        )
        got_a.append(to_hi(sent.astype(BF16)))
    coef_t = turned(coefs)

    tables = jnp.asarray(dft_matrices(window))
    grad_a, grad_b = far_gradient(
        tables, own_amp, moved_amp, odd_row, live,
        low, high, (mine_loc, got_loc, rem_own, *got_a, near_mid, cross_mid),
    )

    a_hi = to_hi(grad_a)
    rem = to_strip(grad_a)
    rem_hi = to_strip(a_hi)
    near, cross = to_near(grad_b), to_cross(grad_b)
    pieces = []
    for own, other in ((rem, rem_hi), (grad_a, a_hi), (near, cross)):
        pieces += [own, other, to_core(own), to_core(other)]
    return backward_gradient(coef_t, low, high, pieces, parts, beams)


def solution(mesh):
    return jax.shard_map(
        body,
        mesh=mesh,
        in_specs=(
            P(None, "beam", "scan", None),
            P(None, "beam"),
            P(None, "beam"),
            P("scan"),
            P("scan"),
            P("scan"),
            P("scan", None, None),
        ),
        out_specs=P(None, "beam", "scan", None),
        check_vma=False,
    )
```
